256 devices in a mesh: af: 4 (over z_hi), xr: 4 (over x), xc: 16 (over y, z_lo, core).
Axes of the slice: x: 4, y: 4, z: 8 (z_hi: 4, z_lo: 2; z = z_hi * 2 + z_lo), core: 2. Of those that a mesh axis runs over, the one named last changes fastest.
Arguments:
- samples: int32 [4096, 77824], P(('xr', 'xc', 'af')), may hold values from -8 to 7
- kept_channels: int32 [32], replicated, may hold values from 1 to 2047
- flags: int32 [4096], P(('xr', 'xc', 'af')), may hold values 0 or 1
Outputs:
- visibilities: bfloat16 [32, 2, 4096, 4096], P('af', None, 'xr', 'xc')
The draws below stay inside these ranges and needn't reach their ends.
All inputs are finite; a program needn't handle non-finite values. No bound on the sum of `flags` on one device may be relied on, other than what follows from the above.
Results may differ from the reference program's by a relative error of at most 0.001.
Values sent between devices are 32-bit elements; how exact they have to be, the bound alone decides.
A program may use at most 64 MiB of HBM per device.

```python
import jax
import jax.numpy as jnp
from jax import lax

NFFT = 4096
TAPS = 4
SPEC = 16
CHK = 32
INP = 4096
PIECE = 64
N_XR = 4
N_XC = 16


def set_ends(array, stream_key, least, top_value):
    dims = array.shape
    place = [jax.random.randint(jax.random.fold_in(stream_key, axis), (), 0, dims[axis]) for axis in range(len(dims))]
    array = array.at[tuple(place)].set(least)
    longest = dims.index(max(dims))
    place[longest] = (place[longest] + 1) % dims[longest]
    return array.at[tuple(place)].set(top_value)


def setup_inputs(seed: int = 0) -> dict:
    key_list = jax.random.split(jax.random.key(seed), 4)
    samples = set_ends(jax.random.randint(key_list[0], (INP, (SPEC + TAPS - 1) * NFFT), -8, 8), jax.random.fold_in(key_list[0], 1), -8, 7).astype(jnp.int32)
    kept_channels = set_ends(jax.random.randint(key_list[1], (CHK,), 1, NFFT // 2), jax.random.fold_in(key_list[1], 1), 1, (NFFT // 2) - 1).astype(jnp.int32)
    flags = set_ends((jax.random.randint(key_list[2], (INP,), 0, 8) < 7).astype(jnp.int32), jax.random.fold_in(key_list[2], 1), 0, 1)
    return {"samples": samples, "kept_channels": kept_channels, "flags": flags}


def window_table(kept_channels, nfft, taps):
    length = taps * nfft
    points = jnp.arange(length, dtype=jnp.float32)
    window = jnp.sinc((points - length / 2 + 0.5) / nfft) * (0.5 - 0.5 * jnp.cos(2.0 * jnp.pi * (points + 0.5) / length))
    window = window * (0.25 / jnp.sqrt(jnp.sum(window * window)))
    offsets = jnp.arange(nfft, dtype=jnp.int32)
    phases = kept_channels.astype(jnp.int32)[:, None] * offsets[None, :] % nfft
    radians = 2.0 * jnp.pi / nfft * phases.astype(jnp.float32)
    shaped = window.reshape(taps, nfft)
    cosine = shaped[:, None, :] * jnp.cos(radians)[None]
    sine = -shaped[:, None, :] * jnp.sin(radians)[None]
    return jnp.stack([cosine, sine], axis=1)

def channelize(samples, flags, filter_table, spec_count):
    taps = filter_table.shape[0]
    nfft = filter_table.shape[3]
    inputs = samples.shape[0]
    blocks = samples.astype(jnp.float32).reshape(inputs, spec_count + taps - 1, nfft)
    summed = jnp.zeros((filter_table.shape[2], inputs, 2, spec_count), jnp.float32)
    for tap_index in range(taps):
        frames = blocks[:, tap_index:tap_index + spec_count, :]
        summed = summed + jnp.einsum('pcn,isn->cips', filter_table[tap_index], frames, precision=lax.Precision.HIGHEST)
    summed = summed * flags.astype(jnp.float32)[None, :, None, None]
    return summed.reshape(summed.shape[0], inputs * 2 * spec_count)

def correlate(row_block, col_block, spec_count):
    real_part = col_block[..., :spec_count]
    imag_part = col_block[..., spec_count:]
    paired = jnp.concatenate([col_block, jnp.concatenate([-imag_part, real_part], axis=-1)], axis=1)
    product = jnp.einsum('cis,cjs->cij', row_block, paired, precision=lax.Precision.HIGHEST) * (1.0 / spec_count)
    col_count = col_block.shape[1]
    return jnp.stack([product[..., :col_count], product[..., col_count:]], axis=1).astype(jnp.bfloat16)

def reference(samples, kept_channels, flags):
    filter_table = window_table(kept_channels, NFFT, TAPS)
    group_count = INP // PIECE
    grouped = samples.reshape(group_count, PIECE, samples.shape[1])
    grouped_flags = flags.reshape(group_count, PIECE)
    spectra = lax.map(lambda pair: channelize(pair[0], pair[1], filter_table, SPEC), (grouped, grouped_flags))
    spectra = spectra.reshape(group_count, CHK, PIECE, 2 * SPEC).transpose(1, 0, 2, 3).reshape(CHK, INP, 2 * SPEC)
    columns = jnp.arange(INP, dtype=jnp.int32)
    col_group = columns // (N_XR * PIECE)
    row_group = columns // PIECE % N_XR
    inside = columns % PIECE
    source = (row_group * (N_XC * PIECE) + col_group * PIECE + inside).astype(jnp.int32)
    permuted = jnp.take(spectra, source, axis=1)
    return lax.map(lambda pair: correlate(pair[0][None], pair[1][None], SPEC)[0], (spectra, permuted))
```

```python
import functools
import math

import jax
import jax.numpy as jnp
from jax import lax
from jax.experimental import pallas as pl
from jax.experimental.pallas import tpu as pltpu
from jax.sharding import PartitionSpec as P

NFFT = 4096
TAPS = 4
SPEC = 16
BLOCKS = SPEC + TAPS - 1
CHUNKS = 4
CHUNK = NFFT // CHUNKS
MESH = pl.DeviceIdType.MESH
NT = (((1,), (1,)), ((), ()))


def sincos(phase, period):
    quarter = period // 4
    turned = phase + quarter // 2
    rest = (turned & (quarter - 1)) - quarter // 2
    quadrant = lax.shift_right_logical(turned, int(math.log2(quarter))) & 3
    angle = rest.astype(jnp.float32) * (2.0 * math.pi / period)
    z = angle * angle
    s = angle * (1.0 + z * (-1.0 / 6 + z * (1.0 / 120 + z * (-1.0 / 5040 + z * (1.0 / 362880)))))
    c = 1.0 + z * (-0.5 + z * (1.0 / 24 + z * (-1.0 / 720 + z * (1.0 / 40320))))
    odd = (quadrant & 1) == 1
    sine = jnp.where(odd, c, s)
    cosine = jnp.where(odd, s, c)
    sine = jnp.where(quadrant >= 2, -sine, sine)
    cosine = jnp.where((quadrant == 1) | (quadrant == 2), -cosine, cosine)
    return sine, cosine


def spread(
    samples, kept, flags, rows, cols, raw, frames, table, window, blocks,
    load_sem, turn_send, turn_recv, row_send, row_recv, col_send, col_recv,
):
    f, r, k = lax.axis_index("af"), lax.axis_index("xr"), lax.axis_index("xc")
    y, zl, core = k // 4, (k // 2) % 2, k % 2

    for part in range(CHUNKS):
        for b in range(BLOCKS):
            pltpu.make_async_copy(
                samples.at[:, pl.ds(b * NFFT + part * CHUNK, CHUNK)], raw.at[part, b], load_sem.at[part]
            ).start()

    def slot(yy, zz, cc):
        return (yy * 2 + zz) * 2 + cc

    y_peers = [slot((y + d) % 4, zl, core) for d in (1, 3, 2)]
    z_peer = slot(y, 1 - zl, core)
    c_peer = slot(y, zl, 1 - core)
    x_peers = [(r + d) % 4 for d in (1, 3, 2)]
    f_peers = [(f + d) % 4 for d in (1, 3, 2)]

    barrier = pltpu.get_barrier_semaphore()
    for peer in f_peers:
        pl.semaphore_signal(barrier, inc=1, device_id={"af": peer}, device_id_type=MESH)
    for peer in x_peers:
        pl.semaphore_signal(barrier, inc=1, device_id={"xr": peer}, device_id_type=MESH)
    for peer in y_peers + [z_peer, c_peer]:
        pl.semaphore_signal(barrier, inc=1, device_id={"xc": peer}, device_id_type=MESH)

    lane = lax.broadcasted_iota(jnp.int32, (64, 128), 1)
    line = lax.broadcasted_iota(jnp.int32, (64, 128), 0)
    channel = ((line >> 2) & 7) * 4 + (line >> 5) * 2 + ((line >> 1) & 1)
    kept_line = jnp.zeros((64, 128), jnp.int32)
    for j in range(32):
        kept_line = jnp.where(channel == j, kept[j], kept_line)
    quarter_turn = (line & 1) * (NFFT // 4)
    coarse_s, coarse_c = sincos((kept_line * (128 * (lane & 31)) + quarter_turn) & (NFFT - 1), NFFT)
    fine_s, fine_c = sincos((kept_line * lane) & (NFFT - 1), NFFT)

    odd = (
        2 * (lax.broadcasted_iota(jnp.int32, (128, 128), 0) * 128 + lax.broadcasted_iota(jnp.int32, (128, 128), 1))
        - (TAPS * NFFT - 1)
    )
    ws, wc = sincos(odd & (8 * NFFT - 1), 8 * NFFT)
    shape = ws * wc / (odd.astype(jnp.float32) * (2.0 * math.pi / (8 * NFFT))) * (0.5 + 0.5 * wc)
    window[...] = shape
    total = jnp.sum(jnp.sum(shape * shape, axis=0, keepdims=True), axis=1, keepdims=True)
    scale = 0.25 * lax.rsqrt(total)

    summed = None
    for part in range(CHUNKS):
        for a in range(part * CHUNK // 128, (part + 1) * CHUNK // 128):
            trig = coarse_c[:, a : a + 1] * fine_c - coarse_s[:, a : a + 1] * fine_s
            for t in range(TAPS):
                value = trig * window[t * 32 + a : t * 32 + a + 1, :]
                high = value.astype(jnp.bfloat16)
                low = (value - high.astype(jnp.float32)).astype(jnp.bfloat16)
                for half in range(2):
                    at = (t // 2) * 128 + half * 64 + (t % 2) * 32
                    table[at : at + 32, a * 128 : (a + 1) * 128] = high[half * 32 : half * 32 + 32]
                    table[256 + at : 256 + at + 32, a * 128 : (a + 1) * 128] = low[half * 32 : half * 32 + 32]
        pltpu.make_async_copy(raw.at[part], raw.at[part], load_sem.at[part]).wait()
        span = slice(part * CHUNK, (part + 1) * CHUNK)
        for b in range(BLOCKS):
            frames[b * 16 : (b + 1) * 16, span] = raw[part, b].astype(jnp.float32).astype(jnp.bfloat16)
        product = lax.dot_general(frames[:, span], table[:, span], NT, preferred_element_type=jnp.float32)
        summed = product if summed is None else summed + product

    summed = summed[:, :256] + summed[:, 256:]
    first, second = summed[:, :128], summed[:, 128:]
    wide_lane = lax.broadcasted_iota(jnp.int32, (256, 128), 1)
    tapped = jnp.where(
        (wide_lane & 32) == 0, first[0:256] + second[32:288], first[16:272] + second[48:304]
    )
    lane = lax.broadcasted_iota(jnp.int32, (128, 128), 1)
    low_tap = (lane & 32) == 0
    early, late = tapped[:128], tapped[128:]
    crossed = jnp.where(low_tap, late, early)
    crossed = jnp.where(low_tap, pltpu.roll(crossed, 96, 1), pltpu.roll(crossed, 32, 1))
    both = jnp.where(low_tap, early, late) + crossed
    tiles = [both[16 * j : 16 * j + 16] for j in range(8)]
    lane = lax.broadcasted_iota(jnp.int32, (16, 128), 1)
    for bit in range(3):
        step = 4 << bit
        low_lane = (lane & step) == 0
        for j in range(8):
            if j & (1 << bit):
                continue
            zero, one = tiles[j], tiles[j | (1 << bit)]
            tiles[j] = jnp.where(low_lane, zero, pltpu.roll(one, step, 1))
            tiles[j | (1 << bit)] = jnp.where(low_lane, pltpu.roll(zero, 128 - step, 1), one)
    row = lax.broadcasted_iota(jnp.int32, (16, 128), 0)
    gain = jnp.zeros((16, 128), jnp.int32)
    for j in range(16):
        gain = jnp.where(row == j, flags[j], gain)
    gain = gain.astype(jnp.float32) * scale
    for j in range(8):
        blocks[j // 2, j % 2] = tiles[j] * gain

    pl.semaphore_wait(barrier, 11)

    def turn(d, peer):
        return pltpu.make_async_remote_copy(
            src_ref=blocks.at[peer],
            dst_ref=rows.at[k, :, pl.ds(pl.multiple_of(f * 16, 16), 16), :],
            send_sem=turn_send.at[d],
            recv_sem=turn_recv.at[d],
            device_id={"af": peer},
            device_id_type=MESH,
        )

    turns = [turn(d, peer) for d, peer in enumerate(f_peers)]
    for copy in turns:
        copy.start()
    rows[k, :, pl.ds(pl.multiple_of(f * 16, 16), 16), :] = blocks[f]
    for copy in turns:
        copy.wait()

    def spread_row(number, which, peer):
        return pltpu.make_async_remote_copy(
            src_ref=rows.at[which],
            dst_ref=rows.at[which],
            send_sem=row_send.at[number],
            recv_sem=row_recv.at[number],
            device_id={"xc": peer},
            device_id_type=MESH,
        )

    def spread_col(number, peer):
        return pltpu.make_async_remote_copy(
            src_ref=rows.at[k],
            dst_ref=cols.at[r],
            send_sem=col_send.at[number],
            recv_sem=col_recv.at[number],
            device_id={"xr": peer},
            device_id_type=MESH,
        )

    started = []

    def go(copy):
        copy.start()
        started.append(copy)
        return copy

    along_y = [go(spread_row(n, k, peer)) for n, peer in enumerate(y_peers)]
    along_z = [go(spread_row(3, k, z_peer))]
    between = [go(spread_row(7, k, c_peer))]
    along_x = [go(spread_col(n, peer)) for n, peer in enumerate(x_peers)]
    cols[r] = rows[k]
    sources = [slot((y - d) % 4, zl, core) for d in (1, 3, 2)]
    for n, source in enumerate(sources):
        along_y[n].wait_recv()
        along_z.append(go(spread_row(4 + n, source, z_peer)))
        between.append(go(spread_row(8 + n, source, c_peer)))
    partners = [slot(y, 1 - zl, core)] + [slot((y - d) % 4, 1 - zl, core) for d in (1, 3, 2)]
    for n, source in enumerate(partners):
        along_z[n].wait_recv()
        between.append(go(spread_row(11 + n, source, c_peer)))
    for copy in between + along_x:
        copy.wait_recv()
    for copy in started:
        copy.wait_send()


def correlate(rows, cols, out, left, stage, out_sem):
    lane = lax.broadcasted_iota(jnp.int32, (256, 128), 1)
    real_lane = (lane & 1) == 0

    def step(number, _):
        c_hi, p = number // 2, number % 2
        long_lane = lax.broadcasted_iota(jnp.int32, (1024, 128), 1)
        x = rows[:, c_hi].reshape(1024, 128)
        high = x.astype(jnp.bfloat16)
        low = (x - high.astype(jnp.float32)).astype(jnp.bfloat16)
        left[:, :128] = jnp.where((long_lane >> 6) == p, x, pltpu.roll(x, 64, 1)).astype(jnp.bfloat16)
        left[:, 128:] = low
        operand = left[...]
        mine = (lane >> 6) == p
        c = cols[:, c_hi].reshape(256, 128) * (1.0 / SPEC)
        c = jnp.where(mine, c, pltpu.roll(c, 64, 1))
        swapped = jnp.where(real_lane, -pltpu.roll(c, 127, 1), pltpu.roll(c, 1, 1))
        for part, value in enumerate((c, swapped)):
            value_high = value.astype(jnp.bfloat16).astype(jnp.float32)
            value_low = value - value_high
            first = jnp.where(lane < 64, value_high, value_low)
            for e in range(2):
                mask = ((lane >> 1) & 1) == e
                right = jnp.concatenate(
                    [jnp.where(mask, first, 0.0), jnp.where(mask & mine, value_high, 0.0)], axis=1
                ).astype(jnp.bfloat16)
                product = lax.dot_general(operand, right, NT, preferred_element_type=jnp.float32)
                channel = number * 2 + e
                stage[channel, part] = product.astype(jnp.bfloat16)
                pltpu.make_async_copy(
                    stage.at[channel, part], out.at[channel, part], out_sem.at[channel, part]
                ).start()
        return 0

    lax.fori_loop(0, 4, step, 0)

    def finish(channel, _):
        for part in range(2):
            pltpu.make_async_copy(
                stage.at[channel, part], out.at[channel, part], out_sem.at[channel, part]
            ).wait()
        return 0

    lax.fori_loop(0, 8, finish, 0)


def shards(samples, kept_channels, flags):
    vmem = pl.BlockSpec(memory_space=pltpu.VMEM)
    smem = pl.BlockSpec(memory_space=pltpu.SMEM)
    hbm = pl.BlockSpec(memory_space=pl.ANY)
    dma = pltpu.SemaphoreType.DMA
    rows, cols = pl.pallas_call(
        spread,
        out_shape=[pltpu.VMEM((16, 2, 64, 128), jnp.float32), pltpu.VMEM((4, 2, 64, 128), jnp.float32)],
        in_specs=[hbm, smem, smem],
        out_specs=[vmem, vmem],
        scratch_shapes=[
            pltpu.VMEM((CHUNKS, BLOCKS, 16, CHUNK), jnp.int32),
            pltpu.VMEM((BLOCKS * 16, NFFT), jnp.bfloat16),
            pltpu.VMEM((512, NFFT), jnp.bfloat16),
            pltpu.VMEM((128, 128), jnp.float32),
            pltpu.VMEM((4, 2, 16, 128), jnp.float32),
            dma((CHUNKS,)),
            dma((3,)),
            dma((3,)),
            dma((15,)),
            dma((15,)),
            dma((3,)),
            dma((3,)),
        ],
        compiler_params=pltpu.CompilerParams(
            collective_id=0, has_side_effects=True, vmem_limit_bytes=40 * 1024 * 1024
        ),
        name="spread",
    )(samples, kept_channels, flags)
    return pl.pallas_call(
        correlate,
        out_shape=jax.ShapeDtypeStruct((8, 2, 1024, 256), jnp.bfloat16),
        in_specs=[vmem, vmem],
        out_specs=hbm,
        scratch_shapes=[
            pltpu.VMEM((1024, 256), jnp.bfloat16),
            pltpu.VMEM((8, 2, 1024, 256), jnp.bfloat16),
            dma((8, 2)),
        ],
        compiler_params=pltpu.CompilerParams(vmem_limit_bytes=40 * 1024 * 1024),
        name="correlate",
    )(rows, cols)


def solution(mesh):
    return jax.shard_map(
        shards,
        mesh=mesh,
        in_specs=(P(("xr", "xc", "af"), None), P(), P(("xr", "xc", "af"))),
        out_specs=P("af", None, "xr", "xc"),
        check_vma=False,
    )
```

```python
import functools
import math

import jax
import jax.numpy as jnp
from jax import lax
from jax.experimental import pallas as pl
from jax.experimental.pallas import tpu as pltpu
from jax.sharding import PartitionSpec as P

NFFT = 4096
TAPS = 4
SPEC = 16
BLOCKS = SPEC + TAPS - 1
CHUNKS = 4
CHUNK = NFFT // CHUNKS
MESH = pl.DeviceIdType.MESH
NT = (((1,), (1,)), ((), ()))
UNITS = (
    ((0, 0), (1, 1), (7, 1), (1, 0), (7, 0), (6, 1), (6, 0), (2, 0)),
    ((0, 1), (2, 1), (3, 1), (5, 1), (3, 0), (5, 0), (4, 1), (4, 0)),
)
Z_ORDER = (4, 3, 5, 2, 6, 1, 7)
ARRIVALS = (
    ("z", 1), ("z", 2), ("y", 1, 0), ("y", 3, 0), ("z", 3), ("z", 4), ("y", 2, 0), ("z", 5), ("z", 6), ("z", 7),
    *(("y", dy, j) for j in range(1, 8) for dy in (1, 3, 2)),
)


def sincos(phase, period):
    quarter = period // 4
    turned = phase + quarter // 2
    rest = (turned & (quarter - 1)) - quarter // 2
    quadrant = lax.shift_right_logical(turned, int(math.log2(quarter))) & 3
    angle = rest.astype(jnp.float32) * (2.0 * math.pi / period)
    z = angle * angle
    s = angle * (1.0 + z * (-1.0 / 6 + z * (1.0 / 120 + z * (-1.0 / 5040 + z * (1.0 / 362880)))))
    c = 1.0 + z * (-0.5 + z * (1.0 / 24 + z * (-1.0 / 720 + z * (1.0 / 40320))))
    odd = (quadrant & 1) == 1
    sine = jnp.where(odd, c, s)
    cosine = jnp.where(odd, s, c)
    sine = jnp.where(quadrant >= 2, -sine, sine)
    cosine = jnp.where((quadrant == 1) | (quadrant == 2), -cosine, cosine)
    return sine, cosine


def spread(
    samples, kept_hbm, flags_hbm, rows, cols, raw, frames, table, window, blocks, kept, flags,
    load_sem, small_sem, z_send, z_recv, y_send, y_recv, c_send, c_recv, x_send, x_recv,
):
    f, r, k = lax.axis_index("af"), lax.axis_index("xr"), lax.axis_index("xc")
    y, zl, core = k // 4, (k // 2) % 2, k % 2
    z = f * 2 + zl

    small = [
        pltpu.make_async_copy(kept_hbm, kept, small_sem.at[0]),
        pltpu.make_async_copy(flags_hbm, flags, small_sem.at[1]),
    ]
    for copy in small:
        copy.start()
    for part in range(CHUNKS):
        for b in range(BLOCKS):
            pltpu.make_async_copy(
                samples.at[:, pl.ds(b * NFFT + part * CHUNK, CHUNK)], raw.at[part, b], load_sem.at[part]
            ).start()

    def pick(pair):
        return pair[0] if pair[0] == pair[1] else pair[0] + core * (pair[1] - pair[0])

    def on_z(d, cc):
        zz = (z + d) % 8
        return {"af": zz // 2, "xc": y * 4 + (zz % 2) * 2 + cc}

    y_peers = {d: {"xc": ((y + d) % 4) * 4 + zl * 2 + core} for d in (1, 3, 2)}
    c_peer = {"xc": k + 1 - 2 * core}

    def on_x(d, cc):
        return {"xr": (r + d) % 4, "xc": y * 4 + zl * 2 + cc}

    barrier = pltpu.get_barrier_semaphore()
    greeted = [on_z(d, cc) for d in range(1, 8) for cc in range(2)] + [on_x(d, cc) for d in range(1, 4) for cc in range(2)]
    greeted += [*y_peers.values(), c_peer]
    for peer in greeted:
        pl.semaphore_signal(barrier, inc=1, device_id=peer, device_id_type=MESH)

    odd = (
        2 * (lax.broadcasted_iota(jnp.int32, (128, 128), 0) * 128 + lax.broadcasted_iota(jnp.int32, (128, 128), 1))
        - (TAPS * NFFT - 1)
    )
    ws, wc = sincos(odd & (8 * NFFT - 1), 8 * NFFT)
    shape = ws * wc / (odd.astype(jnp.float32) * (2.0 * math.pi / (8 * NFFT))) * (0.5 + 0.5 * wc)
    window[...] = shape
    total = jnp.sum(jnp.sum(shape * shape, axis=0, keepdims=True), axis=1, keepdims=True)
    scale = 0.25 * lax.rsqrt(total)

    for copy in small:
        copy.wait()

    lane = lax.broadcasted_iota(jnp.int32, (64, 128), 1)
    line = lax.broadcasted_iota(jnp.int32, (64, 128), 0)
    channel = ((line >> 2) & 7) * 4 + (line >> 5) * 2 + ((line >> 1) & 1)
    kept_line = jnp.zeros((64, 128), jnp.int32)
    for j in range(32):
        kept_line = jnp.where(channel == j, kept[j], kept_line)
    quarter_turn = (line & 1) * (NFFT // 4)
    coarse_s, coarse_c = sincos((kept_line * (128 * (lane & 31)) + quarter_turn) & (NFFT - 1), NFFT)
    fine_s, fine_c = sincos((kept_line * lane) & (NFFT - 1), NFFT)

    summed = None
    for part in range(CHUNKS):
        for a in range(part * CHUNK // 128, (part + 1) * CHUNK // 128):
            trig = coarse_c[:, a : a + 1] * fine_c - coarse_s[:, a : a + 1] * fine_s
            for t in range(TAPS):
                value = trig * window[t * 32 + a : t * 32 + a + 1, :]
                high = value.astype(jnp.bfloat16)
                low = (value - high.astype(jnp.float32)).astype(jnp.bfloat16)
                for half in range(2):
                    at = (t // 2) * 128 + half * 64 + (t % 2) * 32
                    table[at : at + 32, a * 128 : (a + 1) * 128] = high[half * 32 : half * 32 + 32]
                    table[256 + at : 256 + at + 32, a * 128 : (a + 1) * 128] = low[half * 32 : half * 32 + 32]
        pltpu.make_async_copy(raw.at[part], raw.at[part], load_sem.at[part]).wait()
        span = slice(part * CHUNK, (part + 1) * CHUNK)
        for b in range(BLOCKS):
            frames[b * 16 : (b + 1) * 16, span] = raw[part, b].astype(jnp.float32).astype(jnp.bfloat16)
        product = lax.dot_general(frames[:, span], table[:, span], NT, preferred_element_type=jnp.float32)
        summed = product if summed is None else summed + product

    summed = summed[:, :256] + summed[:, 256:]
    first, second = summed[:, :128], summed[:, 128:]
    wide_lane = lax.broadcasted_iota(jnp.int32, (256, 128), 1)
    tapped = jnp.where(
        (wide_lane & 32) == 0, first[0:256] + second[32:288], first[16:272] + second[48:304]
    )
    lane = lax.broadcasted_iota(jnp.int32, (128, 128), 1)
    low_tap = (lane & 32) == 0
    early, late = tapped[:128], tapped[128:]
    crossed = jnp.where(low_tap, late, early)
    crossed = jnp.where(low_tap, pltpu.roll(crossed, 96, 1), pltpu.roll(crossed, 32, 1))
    both = jnp.where(low_tap, early, late) + crossed
    tiles = [both[16 * j : 16 * j + 16] for j in range(8)]
    lane = lax.broadcasted_iota(jnp.int32, (16, 128), 1)
    for bit in range(3):
        step = 4 << bit
        low_lane = (lane & step) == 0
        for j in range(8):
            if j & (1 << bit):
                continue
            zero, one = tiles[j], tiles[j | (1 << bit)]
            tiles[j] = jnp.where(low_lane, zero, pltpu.roll(one, step, 1))
            tiles[j | (1 << bit)] = jnp.where(low_lane, pltpu.roll(zero, 128 - step, 1), one)
    row = lax.broadcasted_iota(jnp.int32, (16, 128), 0)
    gain = jnp.zeros((16, 128), jnp.int32)
    for j in range(16):
        gain = jnp.where(row == j, flags[j], gain)
    gain = gain.astype(jnp.float32) * scale
    for j in range(8):
        blocks[j // 2, j % 2] = tiles[j] * gain

    pl.semaphore_wait(barrier, len(greeted))

    started = []

    def copy_to(src, dst, sems, send_at, recv_at, peer):
        return pltpu.make_async_remote_copy(
            src_ref=src,
            dst_ref=dst,
            send_sem=sems[0].at[send_at],
            recv_sem=sems[1].at[recv_at],
            device_id=peer,
            device_id_type=MESH,
        )

    def send(src, dst, sems, at, peer):
        copy = copy_to(src, dst, sems, at, at, peer)
        copy.start()
        started.append(copy)
        return copy

    def arrived(block, sem):
        pltpu.make_async_copy(block, block, sem).wait()

    def place(ref, dy, dz, cc):
        yy, zz = (y - dy) % 4, (z - dz) % 8
        return ref.at[yy, zz % 2, cc, zz // 2]

    def unit(j):
        return tuple(pick((UNITS[0][j][n], UNITS[1][j][n])) for n in range(2))

    along_y, across = {}, {}
    mine = place(rows, 0, 0, core)
    for d in Z_ORDER:
        hosts = [next((cc, j) for cc in range(2) for j in range(8) if UNITS[cc][j] == (d, source)) for source in range(2)]
        copy = copy_to(
            blocks.at[((z + d) % 8) // 2],
            mine,
            (z_send, z_recv),
            (d,),
            (pick((hosts[0][1], hosts[1][1])),),
            on_z(d, pick((hosts[0][0], hosts[1][0]))),
        )
        copy.start()
        started.append(copy)
    mine[...] = blocks[f]

    def to_columns(j, d, slot):
        dz, source = unit(j)
        return copy_to(
            place(rows, 0, dz, source),
            cols.at[r, ((z - dz) % 8) // 2],
            (x_send, x_recv),
            (d, slot),
            (d, dz // 2),
            on_x(d, source),
        )

    def forward(j):
        block = place(rows, 0, *unit(j))
        for d, peer in y_peers.items():
            along_y[d, j] = send(block, block, (y_send, y_recv), (d, j), peer)
        slots = [
            [i for i in range(8) if UNITS[cc][i][0] % 2 == 0].index(j) if UNITS[cc][j][0] % 2 == 0 else None
            for cc in range(2)
        ]
        for d in (1, 3, 2):
            if slots[0] == slots[1] and slots[0] is not None:
                to_columns(j, d, slots[0]).start()
            elif slots != [None, None]:
                owner = 0 if slots[1] is None else 1

                @pl.when(core == owner)
                def _():
                    to_columns(j, d, slots[owner]).start()

        share(0, j)

    def share(dy, j):
        block = place(rows, dy, *unit(j))
        across[dy, j] = send(block, block, (c_send, c_recv), (dy, j), c_peer)

    forward(0)
    for event in ARRIVALS:
        if event[0] == "z":
            arrived(place(rows, 0, *unit(event[1])), z_recv.at[event[1]])
            forward(event[1])
        else:
            along_y[event[1:]].wait_recv()
            share(*event[1:])
    for d in (1, 3, 2):
        for i in range(4):
            arrived(cols.at[(r - d) % 4, i], x_recv.at[d, i])
    for copy in across.values():
        copy.wait_recv()
    for d in (0, 2, 6, 4):
        at = ((z - d) % 8) // 2
        cols[r, at] = rows[y, zl, core, at]
    for copy in started:
        copy.wait_send()
    for d in (1, 3, 2):
        for slot in range(4):
            to_columns(0, d, slot).wait_send()


def correlate(rows, cols, out, left, right, stage, out_sem):
    lane = lax.broadcasted_iota(jnp.int32, (256, 128), 1)
    long_lane = lax.broadcasted_iota(jnp.int32, (1024, 128), 1)
    real_lane = (lane & 1) == 0

    def write(channel, part):
        return pltpu.make_async_copy(stage.at[channel, part], out.at[channel, part], out_sem.at[channel, part])

    for c_hi in range(2):
        x = rows[:, :, :, :, c_hi].reshape(1024, 128)
        turned = pltpu.roll(x, 64, 1)
        high = x.astype(jnp.bfloat16)
        left[c_hi, 0] = jnp.where(long_lane < 64, x, turned).astype(jnp.bfloat16)
        left[c_hi, 1] = jnp.where(long_lane < 64, turned, x).astype(jnp.bfloat16)
        left[c_hi, 2] = (x - high.astype(jnp.float32)).astype(jnp.bfloat16)
        c = cols[:, :, c_hi].reshape(256, 128) * (1.0 / SPEC)
        c_turned = pltpu.roll(c, 64, 1)
        for p in range(2):
            mine = (lane >> 6) == p
            operand = jnp.concatenate([left[c_hi, p], left[c_hi, 2]], axis=1)
            straight = jnp.where(mine, c, c_turned)
            swapped = jnp.where(real_lane, -pltpu.roll(straight, 127, 1), pltpu.roll(straight, 1, 1))
            for part, value in enumerate((straight, swapped)):
                value_high = value.astype(jnp.bfloat16).astype(jnp.float32)
                first = jnp.where(lane < 64, value_high, value - value_high)
                second = jnp.where(mine, value_high, 0.0)
                for e in range(2):
                    mask = ((lane >> 1) & 1) == e
                    channel = c_hi * 4 + p * 2 + e
                    right[channel, part] = jnp.concatenate(
                        [jnp.where(mask, first, 0.0), jnp.where(mask, second, 0.0)], axis=1
                    ).astype(jnp.bfloat16)
                    stage[channel, part] = lax.dot_general(
                        operand, right[channel, part], NT, preferred_element_type=jnp.float32
                    ).astype(jnp.bfloat16)
                    write(channel, part).start()
    for channel in range(8):
        for part in range(2):
            write(channel, part).wait()


def shards(samples, kept_channels, flags):
    vmem = pl.BlockSpec(memory_space=pltpu.VMEM)
    hbm = pl.BlockSpec(memory_space=pltpu.HBM)
    dma = pltpu.SemaphoreType.DMA
    rows, cols = pl.pallas_call(
        spread,
        out_shape=[pltpu.VMEM((4, 2, 2, 4, 2, 16, 128), jnp.float32), pltpu.VMEM((4, 4, 2, 16, 128), jnp.float32)],
        in_specs=[hbm, hbm, hbm],
        out_specs=[vmem, vmem],
        scratch_shapes=[
            pltpu.VMEM((CHUNKS, BLOCKS, 16, CHUNK), jnp.int32),
            pltpu.VMEM((BLOCKS * 16, NFFT), jnp.bfloat16),
            pltpu.VMEM((512, NFFT), jnp.bfloat16),
            pltpu.VMEM((128, 128), jnp.float32),
            pltpu.VMEM((4, 2, 16, 128), jnp.float32),
            pltpu.SMEM((32,), jnp.int32),
            pltpu.SMEM((16,), jnp.int32),
            dma((CHUNKS,)),
            dma((2,)),
            dma((8,)),
            dma((8,)),
            dma((4, 8)),
            dma((4, 8)),
            dma((4, 8)),
            dma((4, 8)),
            dma((4, 4)),
            dma((4, 4)),
        ],
        compiler_params=pltpu.CompilerParams(
            collective_id=0, has_side_effects=True, vmem_limit_bytes=40 * 1024 * 1024
        ),
        name="spread",
    )(*[pltpu.with_memory_space_constraint(array, pltpu.HBM) for array in (samples, kept_channels, flags)])
    return pl.pallas_call(
        correlate,
        out_shape=jax.ShapeDtypeStruct((8, 2, 1024, 256), jnp.bfloat16),
        in_specs=[vmem, vmem],
        out_specs=hbm,
        scratch_shapes=[
            pltpu.VMEM((2, 3, 1024, 128), jnp.bfloat16),
            pltpu.VMEM((8, 2, 256, 256), jnp.bfloat16),
            pltpu.VMEM((8, 2, 1024, 256), jnp.bfloat16),
            dma((8, 2)),
        ],
        compiler_params=pltpu.CompilerParams(vmem_limit_bytes=40 * 1024 * 1024),
        name="correlate",
    )(rows, cols)


def solution(mesh):
    return jax.shard_map(
        shards,
        mesh=mesh,
        in_specs=(P(("xr", "xc", "af"), None), P(), P(("xr", "xc", "af"))),
        out_specs=P("af", None, "xr", "xc"),
        check_vma=False,
    )
```

```python
import functools
import math

import jax
import jax.numpy as jnp
from jax import lax
from jax.experimental import pallas as pl
from jax.experimental.pallas import tpu as pltpu
from jax.sharding import PartitionSpec as P

NFFT = 4096
TAPS = 4
SPEC = 16
BLOCKS = SPEC + TAPS - 1
CHUNKS = 4
CHUNK = NFFT // CHUNKS
MESH = pl.DeviceIdType.MESH
NT = (((1,), (1,)), ((), ()))
UNITS = (
    ((0, 0), (1, 1), (7, 1), (1, 0), (7, 0), (6, 1), (6, 0), (2, 0)),
    ((0, 1), (2, 1), (3, 1), (5, 1), (3, 0), (5, 0), (4, 1), (4, 0)),
)
Z_ORDER = (4, 3, 5, 2, 6, 1, 7)
ARRIVALS = (
    ("z", 1), ("z", 2), ("near", 0), ("z", 3), ("z", 4), ("far", 0), ("z", 5), ("z", 6), ("z", 7),
    *((kind, j) for j in range(1, 8) for kind in ("near", "far")),
)


def sincos(phase, period):
    quarter = period // 4
    turned = phase + quarter // 2
    rest = (turned & (quarter - 1)) - quarter // 2
    quadrant = lax.shift_right_logical(turned, int(math.log2(quarter))) & 3
    angle = rest.astype(jnp.float32) * (2.0 * math.pi / period)
    z = angle * angle
    s = angle * (1.0 + z * (-1.0 / 6 + z * (1.0 / 120 + z * (-1.0 / 5040 + z * (1.0 / 362880)))))
    c = 1.0 + z * (-0.5 + z * (1.0 / 24 + z * (-1.0 / 720 + z * (1.0 / 40320))))
    odd = (quadrant & 1) == 1
    sine = jnp.where(odd, c, s)
    cosine = jnp.where(odd, s, c)
    sine = jnp.where(quadrant >= 2, -sine, sine)
    cosine = jnp.where((quadrant == 1) | (quadrant == 2), -cosine, cosine)
    return sine, cosine


def spread(
    samples, kept_hbm, flags_hbm, rows, cols, raw, frames, table, window, blocks, kept, flags,
    load_sem, small_sem, z_send, z_recv, y_send, y_recv, c_send, c_recv, x_send, x_recv,
):
    f, r, k = lax.axis_index("af"), lax.axis_index("xr"), lax.axis_index("xc")
    y, zl, core = lax.div(k, 4), lax.rem(lax.div(k, 2), 2), lax.rem(k, 2)
    z = f * 2 + zl

    small = [
        pltpu.make_async_copy(kept_hbm, kept, small_sem.at[0]),
        pltpu.make_async_copy(flags_hbm, flags, small_sem.at[1]),
    ]
    for copy in small:
        copy.start()
    for part in range(CHUNKS):
        for b in range(BLOCKS):
            pltpu.make_async_copy(
                samples.at[:, pl.ds(b * NFFT + part * CHUNK, CHUNK)], raw.at[part, b], load_sem.at[part]
            ).start()

    def pick(pair):
        return pair[0] if pair[0] == pair[1] else pair[0] + core * (pair[1] - pair[0])

    def on_z(d, cc):
        zz = lax.rem(z + d, 8)
        return {"af": lax.div(zz, 2), "xc": y * 4 + lax.rem(zz, 2) * 2 + cc}

    y_peers = {d: {"xc": lax.rem(y + d, 4) * 4 + zl * 2 + core} for d in (1, 3, 2)}
    c_peer = {"xc": k + 1 - 2 * core}

    def on_x(d, cc):
        return {"xr": lax.rem(r + d, 4), "xc": y * 4 + zl * 2 + cc}

    barrier = pltpu.get_barrier_semaphore()
    greeted = [on_z(d, cc) for d in range(1, 8) for cc in range(2)] + [on_x(d, cc) for d in range(1, 4) for cc in range(2)]
    greeted += [*y_peers.values(), c_peer]
    for peer in greeted:
        pl.semaphore_signal(barrier, inc=1, device_id=peer, device_id_type=MESH)

    odd = (
        2 * (lax.broadcasted_iota(jnp.int32, (128, 128), 0) * 128 + lax.broadcasted_iota(jnp.int32, (128, 128), 1))
        - (TAPS * NFFT - 1)
    )
    ws, wc = sincos(odd & (8 * NFFT - 1), 8 * NFFT)
    shape = ws * wc / (odd.astype(jnp.float32) * (2.0 * math.pi / (8 * NFFT))) * (0.5 + 0.5 * wc)
    window[...] = shape
    total = jnp.sum(jnp.sum(shape * shape, axis=0, keepdims=True), axis=1, keepdims=True)
    scale = 0.25 * lax.rsqrt(total)

    for copy in small:
        copy.wait()

    lane = lax.broadcasted_iota(jnp.int32, (64, 128), 1)
    line = lax.broadcasted_iota(jnp.int32, (64, 128), 0)
    channel = ((line >> 2) & 7) * 4 + (line >> 5) * 2 + ((line >> 1) & 1)
    kept_line = jnp.zeros((64, 128), jnp.int32)
    for j in range(32):
        kept_line = jnp.where(channel == j, kept[j], kept_line)
    quarter_turn = (line & 1) * (NFFT // 4)
    coarse_s, coarse_c = sincos((kept_line * (128 * (lane & 31)) + quarter_turn) & (NFFT - 1), NFFT)
    fine_s, fine_c = sincos((kept_line * lane) & (NFFT - 1), NFFT)

    summed = None
    for part in range(CHUNKS):
        for a in range(part * CHUNK // 128, (part + 1) * CHUNK // 128):
            trig = coarse_c[:, a : a + 1] * fine_c - coarse_s[:, a : a + 1] * fine_s
            for t in range(TAPS):
                value = trig * window[t * 32 + a : t * 32 + a + 1, :]
                high = value.astype(jnp.bfloat16)
                low = (value - high.astype(jnp.float32)).astype(jnp.bfloat16)
                for half in range(2):
                    at = (t // 2) * 128 + half * 64 + (t % 2) * 32
                    table[at : at + 32, a * 128 : (a + 1) * 128] = high[half * 32 : half * 32 + 32]
                    table[256 + at : 256 + at + 32, a * 128 : (a + 1) * 128] = low[half * 32 : half * 32 + 32]
        pltpu.make_async_copy(raw.at[part], raw.at[part], load_sem.at[part]).wait()
        span = slice(part * CHUNK, (part + 1) * CHUNK)
        for b in range(BLOCKS):
            frames[b * 16 : (b + 1) * 16, span] = raw[part, b].astype(jnp.float32).astype(jnp.bfloat16)
        product = lax.dot_general(frames[:, span], table[:, span], NT, preferred_element_type=jnp.float32)
        summed = product if summed is None else summed + product

    summed = summed[:, :256] + summed[:, 256:]
    first, second = summed[:, :128], summed[:, 128:]
    wide_lane = lax.broadcasted_iota(jnp.int32, (256, 128), 1)
    tapped = jnp.where(
        (wide_lane & 32) == 0, first[0:256] + second[32:288], first[16:272] + second[48:304]
    )
    lane = lax.broadcasted_iota(jnp.int32, (128, 128), 1)
    low_tap = (lane & 32) == 0
    early, late = tapped[:128], tapped[128:]
    crossed = jnp.where(low_tap, late, early)
    crossed = jnp.where(low_tap, pltpu.roll(crossed, 96, 1), pltpu.roll(crossed, 32, 1))
    both = jnp.where(low_tap, early, late) + crossed
    tiles = [both[16 * j : 16 * j + 16] for j in range(8)]
    lane = lax.broadcasted_iota(jnp.int32, (16, 128), 1)
    for bit in range(3):
        step = 4 << bit
        low_lane = (lane & step) == 0
        for j in range(8):
            if j & (1 << bit):
                continue
            zero, one = tiles[j], tiles[j | (1 << bit)]
            tiles[j] = jnp.where(low_lane, zero, pltpu.roll(one, step, 1))
            tiles[j | (1 << bit)] = jnp.where(low_lane, pltpu.roll(zero, 128 - step, 1), one)
    row = lax.broadcasted_iota(jnp.int32, (16, 128), 0)
    gain = jnp.zeros((16, 128), jnp.int32)
    for j in range(16):
        gain = jnp.where(row == j, flags[j], gain)
    gain = gain.astype(jnp.float32) * scale
    for j in range(8):
        blocks[j // 2, j % 2] = tiles[j] * gain

    pl.semaphore_wait(barrier, len(greeted))

    def send(src, dst, send_sem, recv_sem, peer):
        pltpu.make_async_remote_copy(
            src_ref=src,
            dst_ref=dst,
            send_sem=send_sem,
            recv_sem=recv_sem,
            device_id=peer,
            device_id_type=MESH,
        ).start()

    def done(ref, sem):
        pltpu.make_async_copy(ref, ref, sem).wait()

    def place(ref, dy, dz, cc):
        yy, zz = lax.rem(y + 4 - dy, 4), lax.rem(z + 8 - dz, 8)
        return ref.at[yy, lax.rem(zz, 2), cc, lax.div(zz, 2)]

    def unit(j):
        return tuple(pick((UNITS[0][j][n], UNITS[1][j][n])) for n in range(2))

    mine = place(rows, 0, 0, core)
    for d in Z_ORDER:
        hosts = [next((cc, j) for cc in range(2) for j in range(8) if UNITS[cc][j] == (d, source)) for source in range(2)]
        send(
            blocks.at[lax.div(lax.rem(z + d, 8), 2)],
            mine,
            z_send,
            z_recv.at[pick((hosts[0][1], hosts[1][1]))],
            on_z(d, pick((hosts[0][0], hosts[1][0]))),
        )
    mine[...] = blocks[f]

    def to_columns(j):
        dz, source = unit(j)
        for d in (1, 3, 2):
            send(
                place(rows, 0, dz, source),
                cols.at[r, lax.div(lax.rem(z + 8 - dz, 8), 2)],
                x_send,
                x_recv,
                on_x(d, source),
            )

    def forward(j):
        block = place(rows, 0, *unit(j))
        for d, peer in y_peers.items():
            send(block, block, y_send, y_recv.at[1 if d == 2 else 0, j], peer)
        even = [UNITS[cc][j][0] % 2 == 0 for cc in range(2)]
        if all(even):
            to_columns(j)
        elif any(even):
            pl.when(core == even.index(True))(lambda: to_columns(j))
        share(0, j)

    def share(dy, j):
        block = place(rows, dy, *unit(j))
        send(block, block, c_send, c_recv, c_peer)

    forward(0)
    for kind, j in ARRIVALS:
        if kind == "z":
            done(place(rows, 0, *unit(j)), z_recv.at[j])
            forward(j)
        elif kind == "near":
            done(raw.at[0, 0:2, :, 0:256], y_recv.at[0, j])
            share(1, j)
            share(3, j)
        else:
            done(raw.at[0, 0:1, :, 0:256], y_recv.at[1, j])
            share(2, j)
    done(raw.at[0, 0:3], x_recv)
    done(raw.at[0, 0:8], c_recv)
    for d in (0, 2, 6, 4):
        at = lax.div(lax.rem(z + 8 - d, 8), 2)
        cols[r, at] = rows[y, zl, core, at]
    done(raw.at[0, 0:7, :, 0:256], z_send)
    done(raw.at[0, 0:6], y_send)
    done(raw.at[0, 0:3], x_send)
    done(raw.at[0, 0:8], c_send)


def correlate(rows, cols, out, left, right, stage, out_sem):
    lane = lax.broadcasted_iota(jnp.int32, (256, 128), 1)
    long_lane = lax.broadcasted_iota(jnp.int32, (1024, 128), 1)
    real_lane = (lane & 1) == 0

    def write(channel, part):
        return pltpu.make_async_copy(stage.at[channel, part], out.at[channel, part], out_sem)

    for c_hi in range(2):
        x = rows[:, :, :, :, c_hi].reshape(1024, 128)
        turned = pltpu.roll(x, 64, 1)
        high = x.astype(jnp.bfloat16)
        left[c_hi, 0] = jnp.where(long_lane < 64, x, turned).astype(jnp.bfloat16)
        left[c_hi, 1] = jnp.where(long_lane < 64, turned, x).astype(jnp.bfloat16)
        left[c_hi, 2] = (x - high.astype(jnp.float32)).astype(jnp.bfloat16)
        c = cols[:, :, c_hi].reshape(256, 128) * (1.0 / SPEC)
        c_turned = pltpu.roll(c, 64, 1)
        for p in range(2):
            mine = (lane >> 6) == p
            operand = jnp.concatenate([left[c_hi, p], left[c_hi, 2]], axis=1)
            straight = jnp.where(mine, c, c_turned)
            swapped = jnp.where(real_lane, -pltpu.roll(straight, 127, 1), pltpu.roll(straight, 1, 1))
            for part, value in enumerate((straight, swapped)):
                value_high = value.astype(jnp.bfloat16).astype(jnp.float32)
                first = jnp.where(lane < 64, value_high, value - value_high)
                second = jnp.where(mine, value_high, 0.0)
                for e in range(2):
                    mask = ((lane >> 1) & 1) == e
                    channel = c_hi * 4 + p * 2 + e
                    right[channel, part] = jnp.concatenate(
                        [jnp.where(mask, first, 0.0), jnp.where(mask, second, 0.0)], axis=1
                    ).astype(jnp.bfloat16)
                    stage[channel, part] = lax.dot_general(
                        operand, right[channel, part], NT, preferred_element_type=jnp.float32
                    ).astype(jnp.bfloat16)
                    write(channel, part).start()
    pltpu.make_async_copy(stage, out, out_sem).wait()


def shards(samples, kept_channels, flags):
    vmem = pl.BlockSpec(memory_space=pltpu.VMEM)
    hbm = pl.BlockSpec(memory_space=pltpu.HBM)
    dma = pltpu.SemaphoreType.DMA
    rows, cols = pl.pallas_call(
        spread,
        out_shape=[pltpu.VMEM((4, 2, 2, 4, 2, 16, 128), jnp.float32), pltpu.VMEM((4, 4, 2, 16, 128), jnp.float32)],
        in_specs=[hbm, hbm, hbm],
        out_specs=[vmem, vmem],
        scratch_shapes=[
            pltpu.VMEM((CHUNKS, BLOCKS, 16, CHUNK), jnp.int32),
            pltpu.VMEM((BLOCKS * 16, NFFT), jnp.bfloat16),
            pltpu.VMEM((512, NFFT), jnp.bfloat16),
            pltpu.VMEM((128, 128), jnp.float32),
            pltpu.VMEM((4, 2, 16, 128), jnp.float32),
            pltpu.SMEM((32,), jnp.int32),
            pltpu.SMEM((16,), jnp.int32),
            dma((CHUNKS,)),
            dma((2,)),
            dma,
            dma((8,)),
            dma,
            dma((2, 8)),
            dma,
            dma,
            dma,
            dma,
        ],
        compiler_params=pltpu.CompilerParams(
            collective_id=0, has_side_effects=True, vmem_limit_bytes=40 * 1024 * 1024
        ),
        name="spread",
    )(*[pltpu.with_memory_space_constraint(array, pltpu.HBM) for array in (samples, kept_channels, flags)])
    return pl.pallas_call(
        correlate,
        out_shape=jax.ShapeDtypeStruct((8, 2, 1024, 256), jnp.bfloat16),
        in_specs=[vmem, vmem],
        out_specs=hbm,
        scratch_shapes=[
            pltpu.VMEM((2, 3, 1024, 128), jnp.bfloat16),
            pltpu.VMEM((8, 2, 256, 256), jnp.bfloat16),
            pltpu.VMEM((8, 2, 1024, 256), jnp.bfloat16),
            dma,
        ],
        compiler_params=pltpu.CompilerParams(vmem_limit_bytes=40 * 1024 * 1024),
        name="correlate",
    )(rows, cols)


def solution(mesh):
    return jax.shard_map(
        shards,
        mesh=mesh,
        in_specs=(P(("xr", "xc", "af"), None), P(), P(("xr", "xc", "af"))),
        out_specs=P("af", None, "xr", "xc"),
        check_vma=False,
    )
```

```python
import functools
import math

import jax
import jax.numpy as jnp
from jax import lax
from jax.experimental import pallas as pl
from jax.experimental.pallas import tpu as pltpu
from jax.sharding import PartitionSpec as P

NFFT = 4096
TAPS = 4
SPEC = 16
BLOCKS = SPEC + TAPS - 1
CHUNKS = 4
CHUNK = NFFT // CHUNKS
MESH = pl.DeviceIdType.MESH
NT = (((1,), (1,)), ((), ()))
UNITS = (
    ((0, 0), (7, 1), (1, 0), (7, 0), (6, 1), (2, 1), (6, 0), (2, 0)),
    ((0, 1), (1, 1), (3, 1), (5, 1), (3, 0), (5, 0), (4, 1), (4, 0)),
)
DIRECT = (1, 7)
Z_ORDER = (4, 3, 5, 2, 6, 1, 7)
ARRIVALS = (
    ("pass", 0), *(("z", j) for j in range(1, 8)), *(("pass", j) for j in (6, 7, 4, 5, 1, 2, 3)),
    *((kind, j) for j in range(8) for kind in ("near", "far")),
)


def sincos(phase, period):
    quarter = period // 4
    turned = phase + quarter // 2
    rest = (turned & (quarter - 1)) - quarter // 2
    quadrant = lax.shift_right_logical(turned, int(math.log2(quarter))) & 3
    angle = rest.astype(jnp.float32) * (2.0 * math.pi / period)
    z = angle * angle
    s = angle * (1.0 + z * (-1.0 / 6 + z * (1.0 / 120 + z * (-1.0 / 5040 + z * (1.0 / 362880)))))
    c = 1.0 + z * (-0.5 + z * (1.0 / 24 + z * (-1.0 / 720 + z * (1.0 / 40320))))
    odd = (quadrant & 1) == 1
    sine = jnp.where(odd, c, s)
    cosine = jnp.where(odd, s, c)
    sine = jnp.where(quadrant >= 2, -sine, sine)
    cosine = jnp.where((quadrant == 1) | (quadrant == 2), -cosine, cosine)
    return sine, cosine


def spread(
    samples, kept_hbm, flags_hbm, rows, cols, raw, frames, table, window, blocks, kept, flags,
    load_sem, small_sem, z_send, z_recv, y_send, y_recv, c_send, c_recv, x_send, x_recv,
):
    f, r, k = lax.axis_index("af"), lax.axis_index("xr"), lax.axis_index("xc")
    y, zl, core = lax.div(k, 4), lax.rem(lax.div(k, 2), 2), lax.rem(k, 2)
    z = f * 2 + zl

    small = [
        pltpu.make_async_copy(kept_hbm, kept, small_sem.at[0]),
        pltpu.make_async_copy(flags_hbm, flags, small_sem.at[1]),
    ]
    for copy in small:
        copy.start()
    for part in range(CHUNKS):
        for b in range(BLOCKS):
            pltpu.make_async_copy(
                samples.at[:, pl.ds(b * NFFT + part * CHUNK, CHUNK)], raw.at[part, b], load_sem.at[part]
            ).start()

    def pick(pair):
        return pair[0] if pair[0] == pair[1] else pair[0] + core * (pair[1] - pair[0])

    def on_z(d, cc):
        zz = lax.rem(z + d, 8)
        return {"af": lax.div(zz, 2), "xc": y * 4 + lax.rem(zz, 2) * 2 + cc}

    y_peers = {d: {"xc": lax.rem(y + d, 4) * 4 + zl * 2 + core} for d in (1, 3, 2)}
    c_peer = {"xc": k + 1 - 2 * core}

    def on_x(d, cc):
        return {"xr": lax.rem(r + d, 4), "xc": y * 4 + zl * 2 + cc}

    barrier = pltpu.get_barrier_semaphore()
    greeted = [on_z(d, cc) for d in range(1, 8) for cc in range(2)] + [on_x(d, cc) for d in range(1, 4) for cc in range(2)]
    greeted += [*y_peers.values(), c_peer]
    for d in DIRECT:
        for cc in range(2):
            for dy in (1, 2, 3):
                peer = on_z(d, cc)
                greeted.append({**peer, "xc": peer["xc"] - y * 4 + lax.rem(y + dy, 4) * 4})
    for peer in greeted:
        pl.semaphore_signal(barrier, inc=1, device_id=peer, device_id_type=MESH)

    odd = (
        2 * (lax.broadcasted_iota(jnp.int32, (128, 128), 0) * 128 + lax.broadcasted_iota(jnp.int32, (128, 128), 1))
        - (TAPS * NFFT - 1)
    )
    ws, wc = sincos(odd & (8 * NFFT - 1), 8 * NFFT)
    shape = ws * wc / (odd.astype(jnp.float32) * (2.0 * math.pi / (8 * NFFT))) * (0.5 + 0.5 * wc)
    window[...] = shape
    total = jnp.sum(jnp.sum(shape * shape, axis=0, keepdims=True), axis=1, keepdims=True)
    scale = 0.25 * lax.rsqrt(total)

    for copy in small:
        copy.wait()

    lane = lax.broadcasted_iota(jnp.int32, (64, 128), 1)
    line = lax.broadcasted_iota(jnp.int32, (64, 128), 0)
    channel = ((line >> 2) & 7) * 4 + (line >> 5) * 2 + ((line >> 1) & 1)
    kept_line = jnp.zeros((64, 128), jnp.int32)
    for j in range(32):
        kept_line = jnp.where(channel == j, kept[j], kept_line)
    quarter_turn = (line & 1) * (NFFT // 4)
    coarse_s, coarse_c = sincos((kept_line * (128 * (lane & 31)) + quarter_turn) & (NFFT - 1), NFFT)
    fine_s, fine_c = sincos((kept_line * lane) & (NFFT - 1), NFFT)

    summed = None
    for part in range(CHUNKS):
        for a in range(part * CHUNK // 128, (part + 1) * CHUNK // 128):
            trig = coarse_c[:, a : a + 1] * fine_c - coarse_s[:, a : a + 1] * fine_s
            for t in range(TAPS):
                value = trig * window[t * 32 + a : t * 32 + a + 1, :]
                high = value.astype(jnp.bfloat16)
                low = (value - high.astype(jnp.float32)).astype(jnp.bfloat16)
                for half in range(2):
                    at = (t // 2) * 128 + half * 64 + (t % 2) * 32
                    table[at : at + 32, a * 128 : (a + 1) * 128] = high[half * 32 : half * 32 + 32]
                    table[256 + at : 256 + at + 32, a * 128 : (a + 1) * 128] = low[half * 32 : half * 32 + 32]
        pltpu.make_async_copy(raw.at[part], raw.at[part], load_sem.at[part]).wait()
        span = slice(part * CHUNK, (part + 1) * CHUNK)
        for b in range(BLOCKS):
            frames[b * 16 : (b + 1) * 16, span] = raw[part, b].astype(jnp.float32).astype(jnp.bfloat16)
        product = lax.dot_general(frames[:, span], table[:, span], NT, preferred_element_type=jnp.float32)
        summed = product if summed is None else summed + product

    summed = summed[:, :256] + summed[:, 256:]
    first, second = summed[:, :128], summed[:, 128:]
    wide_lane = lax.broadcasted_iota(jnp.int32, (256, 128), 1)
    tapped = jnp.where(
        (wide_lane & 32) == 0, first[0:256] + second[32:288], first[16:272] + second[48:304]
    )
    lane = lax.broadcasted_iota(jnp.int32, (128, 128), 1)
    low_tap = (lane & 32) == 0
    early, late = tapped[:128], tapped[128:]
    crossed = jnp.where(low_tap, late, early)
    crossed = jnp.where(low_tap, pltpu.roll(crossed, 96, 1), pltpu.roll(crossed, 32, 1))
    both = jnp.where(low_tap, early, late) + crossed
    tiles = [both[16 * j : 16 * j + 16] for j in range(8)]
    lane = lax.broadcasted_iota(jnp.int32, (16, 128), 1)
    for bit in range(3):
        step = 4 << bit
        low_lane = (lane & step) == 0
        for j in range(8):
            if j & (1 << bit):
                continue
            zero, one = tiles[j], tiles[j | (1 << bit)]
            tiles[j] = jnp.where(low_lane, zero, pltpu.roll(one, step, 1))
            tiles[j | (1 << bit)] = jnp.where(low_lane, pltpu.roll(zero, 128 - step, 1), one)
    row = lax.broadcasted_iota(jnp.int32, (16, 128), 0)
    gain = jnp.zeros((16, 128), jnp.int32)
    for j in range(16):
        gain = jnp.where(row == j, flags[j], gain)
    gain = gain.astype(jnp.float32) * scale
    for j in range(8):
        blocks[j // 2, j % 2] = tiles[j] * gain

    pl.semaphore_wait(barrier, len(greeted))

    def send(src, dst, send_sem, recv_sem, peer):
        pltpu.make_async_remote_copy(
            src_ref=src,
            dst_ref=dst,
            send_sem=send_sem,
            recv_sem=recv_sem,
            device_id=peer,
            device_id_type=MESH,
        ).start()

    def done(ref, sem):
        pltpu.make_async_copy(ref, ref, sem).wait()

    def done_blocks(counts, sem):
        for cc, count in enumerate(counts):
            width = max(n for n in range(1, 5) if count % n == 0)
            like = raw.at[0, 0 : count // width, :, 0 : 256 * width]
            if counts[0] == counts[1]:
                return done(like, sem)
            pl.when(core == cc)(functools.partial(done, like, sem))

    units = [tuple(pick((UNITS[0][j][n], UNITS[1][j][n])) for n in range(2)) for j in range(8)]
    spots = [lax.rem(z + 8 - dz, 8) for dz, _ in units]
    spots = [(lax.rem(zz, 2), source, lax.div(zz, 2)) for zz, (_, source) in zip(spots, units)]
    lines = [lax.rem(y + 4 - dy, 4) for dy in range(4)]

    def place(dy, j):
        return rows.at[(lines[dy], *spots[j])]

    mine = rows.at[y, zl, core, f]
    for d in Z_ORDER:
        hosts = [next((cc, j) for cc in range(2) for j in range(8) if UNITS[cc][j] == (d, source)) for source in range(2)]
        send(
            blocks.at[lax.div(lax.rem(z + d, 8), 2)],
            mine,
            z_send,
            z_recv.at[pick((hosts[0][1], hosts[1][1]))],
            on_z(d, pick((hosts[0][0], hosts[1][0]))),
        )
    for d in DIRECT:
        hosts = [next((cc, j) for cc in range(2) for j in range(8) if UNITS[cc][j] == (d, source)) for source in range(2)]
        host, j = pick((hosts[0][0], hosts[1][0])), pick((hosts[0][1], hosts[1][1]))
        for dy in (2, 1, 3):
            peer = on_z(d, host)
            peer["xc"] = peer["xc"] - y * 4 + lax.rem(y + dy, 4) * 4
            send(blocks.at[lax.div(lax.rem(z + d, 8), 2)], mine, z_send, y_recv.at[1 if dy == 2 else 0, j], peer)
    mine[...] = blocks[f]

    def to_columns(j):
        for d in (1, 3, 2):
            send(place(0, j), cols.at[r, spots[j][2]], x_send, x_recv, on_x(d, spots[j][1]))

    def where(j, test, act):
        passed = [test(UNITS[cc][j][0]) for cc in range(2)]
        if all(passed):
            act()
        elif any(passed):
            pl.when(core == passed.index(True))(act)

    def forward(j):
        block = place(0, j)

        def to_rows():
            for d, peer in y_peers.items():
                send(block, block, y_send, y_recv.at[1 if d == 2 else 0, j], peer)

        where(j, lambda dz: dz not in DIRECT, to_rows)

    def share(dy, j):
        block = place(dy, j)
        send(block, block, c_send, c_recv, c_peer)

    forward(0)
    for kind, j in ARRIVALS:
        if kind == "z":
            done(place(0, j), z_recv.at[j])
            forward(j)
        elif kind == "pass":
            where(j, lambda dz: dz % 2 == 0, lambda: to_columns(j))
            share(0, j)
        elif kind == "near":
            done(raw.at[0, 0:2, :, 0:256], y_recv.at[0, j])
            share(1, j)
            share(3, j)
        else:
            done(raw.at[0, 0:1, :, 0:256], y_recv.at[1, j])
            share(2, j)
    done_blocks((12, 12), x_recv)
    done_blocks((32, 32), c_recv)
    for d in (0, 2, 6, 4):
        at = lax.div(lax.rem(z + 8 - d, 8), 2)
        cols[r, at] = rows[y, zl, core, at]
    done_blocks((7 + 3 * len(DIRECT),) * 2, z_send)
    done_blocks([3 * sum(dz not in DIRECT for dz, _ in units) for units in UNITS], y_send)
    done_blocks([3 * sum(dz % 2 == 0 for dz, _ in units) for units in UNITS], x_send)
    done_blocks((32, 32), c_send)


def correlate(rows, cols, out, left, right, stage, out_sem):
    lane = lax.broadcasted_iota(jnp.int32, (256, 128), 1)
    long_lane = lax.broadcasted_iota(jnp.int32, (1024, 128), 1)
    real_lane = (lane & 1) == 0

    def write(channel, part):
        return pltpu.make_async_copy(stage.at[channel, part], out.at[channel, part], out_sem)

    for c_hi in range(2):
        x = rows[:, :, :, :, c_hi].reshape(1024, 128)
        turned = pltpu.roll(x, 64, 1)
        high = x.astype(jnp.bfloat16)
        left[c_hi, 0] = jnp.where(long_lane < 64, x, turned).astype(jnp.bfloat16)
        left[c_hi, 1] = jnp.where(long_lane < 64, turned, x).astype(jnp.bfloat16)
        left[c_hi, 2] = (x - high.astype(jnp.float32)).astype(jnp.bfloat16)
        c = cols[:, :, c_hi].reshape(256, 128) * (1.0 / SPEC)
        c_turned = pltpu.roll(c, 64, 1)
        for p in range(2):
            mine = (lane >> 6) == p
            operand = jnp.concatenate([left[c_hi, p], left[c_hi, 2]], axis=1)
            straight = jnp.where(mine, c, c_turned)
            swapped = jnp.where(real_lane, -pltpu.roll(straight, 127, 1), pltpu.roll(straight, 1, 1))
            for part, value in enumerate((straight, swapped)):
                value_high = value.astype(jnp.bfloat16).astype(jnp.float32)
                first = jnp.where(lane < 64, value_high, value - value_high)
                second = jnp.where(mine, value_high, 0.0)
                for e in range(2):
                    mask = ((lane >> 1) & 1) == e
                    channel = c_hi * 4 + p * 2 + e
                    right[channel, part] = jnp.concatenate(
                        [jnp.where(mask, first, 0.0), jnp.where(mask, second, 0.0)], axis=1
                    ).astype(jnp.bfloat16)
                    stage[channel, part] = lax.dot_general(
                        operand, right[channel, part], NT, preferred_element_type=jnp.float32
                    ).astype(jnp.bfloat16)
                    write(channel, part).start()
    pltpu.make_async_copy(stage, out, out_sem).wait()


def shards(samples, kept_channels, flags):
    vmem = pl.BlockSpec(memory_space=pltpu.VMEM)
    hbm = pl.BlockSpec(memory_space=pltpu.HBM)
    dma = pltpu.SemaphoreType.DMA
    rows, cols = pl.pallas_call(
        spread,
        out_shape=[pltpu.VMEM((4, 2, 2, 4, 2, 16, 128), jnp.float32), pltpu.VMEM((4, 4, 2, 16, 128), jnp.float32)],
        in_specs=[hbm, hbm, hbm],
        out_specs=[vmem, vmem],
        scratch_shapes=[
            pltpu.VMEM((CHUNKS, BLOCKS, 16, CHUNK), jnp.int32),
            pltpu.VMEM((BLOCKS * 16, NFFT), jnp.bfloat16),
            pltpu.VMEM((512, NFFT), jnp.bfloat16),
            pltpu.VMEM((128, 128), jnp.float32),
            pltpu.VMEM((4, 2, 16, 128), jnp.float32),
            pltpu.SMEM((32,), jnp.int32),
            pltpu.SMEM((16,), jnp.int32),
            dma((CHUNKS,)),
            dma((2,)),
            dma,
            dma((8,)),
            dma,
            dma((2, 8)),
            dma,
            dma,
            dma,
            dma,
        ],
        compiler_params=pltpu.CompilerParams(
            collective_id=0, has_side_effects=True, vmem_limit_bytes=40 * 1024 * 1024
        ),
        name="spread",
    )(*[pltpu.with_memory_space_constraint(array, pltpu.HBM) for array in (samples, kept_channels, flags)])
    return pl.pallas_call(
        correlate,
        out_shape=jax.ShapeDtypeStruct((8, 2, 1024, 256), jnp.bfloat16),
        in_specs=[vmem, vmem],
        out_specs=hbm,
        scratch_shapes=[
            pltpu.VMEM((2, 3, 1024, 128), jnp.bfloat16),
            pltpu.VMEM((8, 2, 256, 256), jnp.bfloat16),
            pltpu.VMEM((8, 2, 1024, 256), jnp.bfloat16),
            dma,
        ],
        compiler_params=pltpu.CompilerParams(vmem_limit_bytes=40 * 1024 * 1024),
        name="correlate",
    )(rows, cols)


def solution(mesh):
    return jax.shard_map(
        shards,
        mesh=mesh,
        in_specs=(P(("xr", "xc", "af"), None), P(), P(("xr", "xc", "af"))),
        out_specs=P("af", None, "xr", "xc"),
        check_vma=False,
    )
```

```python
import functools
import math

import jax
import jax.numpy as jnp
from jax import lax
from jax.experimental import pallas as pl
from jax.experimental.pallas import tpu as pltpu
from jax.sharding import PartitionSpec as P

NFFT = 4096
TAPS = 4
SPEC = 16
BLOCKS = SPEC + TAPS - 1
CHUNKS = 4
EARLY = 0
CHUNK = NFFT // CHUNKS
MESH = pl.DeviceIdType.MESH
NT = (((1,), (1,)), ((), ()))
UNITS = (
    ((0, 0), (7, 1), (1, 0), (7, 0), (6, 1), (2, 1), (6, 0), (2, 0)),
    ((0, 1), (1, 1), (3, 1), (5, 1), (3, 0), (5, 0), (4, 1), (4, 0)),
)
DIRECT = {1: (2, 1, 3), 7: (2, 1, 3), 2: (2,), 6: (2,)}
HALVES = ((4, 3, 5), (2, 6, 1, 7))
SLOTS = {4: (0, 0), 3: (1, 0), 5: (0, 1), 2: (1, 2), 6: (2, 1), 1: (3, 2), 7: (2, 3)}
ARRIVALS = (
    ("pass", 0), *(("z", j) for j in range(1, 8)), *(("pass", j) for j in (6, 7, 4, 5, 1, 2, 3)),
    *((kind, j) for j in range(8) for kind in ("near", "far")),
)


def sincos(phase, period):
    quarter = period // 4
    turned = phase + quarter // 2
    rest = (turned & (quarter - 1)) - quarter // 2
    quadrant = lax.shift_right_logical(turned, int(math.log2(quarter))) & 3
    angle = rest.astype(jnp.float32) * (2.0 * math.pi / period)
    z = angle * angle
    s = angle * (1.0 + z * (-1.0 / 6 + z * (1.0 / 120 + z * (-1.0 / 5040 + z * (1.0 / 362880)))))
    c = 1.0 + z * (-0.5 + z * (1.0 / 24 + z * (-1.0 / 720 + z * (1.0 / 40320))))
    odd = (quadrant & 1) == 1
    sine = jnp.where(odd, c, s)
    cosine = jnp.where(odd, s, c)
    sine = jnp.where(quadrant >= 2, -sine, sine)
    cosine = jnp.where((quadrant == 1) | (quadrant == 2), -cosine, cosine)
    return sine, cosine


def spread(
    samples, kept_hbm, flags_hbm, rows, cols, raw, frames, table, window, blocks, kept, flags,
    load_sem, small_sem, z_send, z_recv, y_send, y_recv, c_send, c_recv, x_send, x_recv,
):
    f, r, k = lax.axis_index("af"), lax.axis_index("xr"), lax.axis_index("xc")
    y, zl, core = lax.div(k, 4), lax.rem(lax.div(k, 2), 2), lax.rem(k, 2)
    z = f * 2 + zl

    small = [
        pltpu.make_async_copy(kept_hbm, kept, small_sem.at[0]),
        pltpu.make_async_copy(flags_hbm, flags, small_sem.at[1]),
    ]
    for copy in small:
        copy.start()
    for part in range(CHUNKS):
        for b in range(BLOCKS):
            pltpu.make_async_copy(
                samples.at[:, pl.ds(b * NFFT + part * CHUNK, CHUNK)], raw.at[part, b], load_sem.at[part]
            ).start()

    def pick(pair):
        return pair[0] if pair[0] == pair[1] else pair[0] + core * (pair[1] - pair[0])

    def on_z(d, cc):
        zz = lax.rem(z + d, 8)
        return {"af": lax.div(zz, 2), "xc": y * 4 + lax.rem(zz, 2) * 2 + cc}

    y_peers = {d: {"xc": lax.rem(y + d, 4) * 4 + zl * 2 + core} for d in (1, 3, 2)}
    c_peer = {"xc": k + 1 - 2 * core}

    def on_x(d, cc):
        return {"xr": lax.rem(r + d, 4), "xc": y * 4 + zl * 2 + cc}

    barrier = pltpu.get_barrier_semaphore()
    greeted = [on_z(d, cc) for d in range(1, 8) for cc in range(2)] + [on_x(d, cc) for d in range(1, 4) for cc in range(2)]
    greeted += [*y_peers.values(), c_peer]
    for d in sorted({*DIRECT, *(8 - d for d in DIRECT)}):
        for cc in range(2):
            for dy in sorted({*DIRECT.get(d, ()), *(4 - dy for dy in DIRECT.get(8 - d, ()))}):
                peer = on_z(d, cc)
                greeted.append({**peer, "xc": peer["xc"] - y * 4 + lax.rem(y + dy, 4) * 4})
    for peer in greeted:
        pl.semaphore_signal(barrier, inc=1, device_id=peer, device_id_type=MESH)

    odd = (
        2 * (lax.broadcasted_iota(jnp.int32, (128, 128), 0) * 128 + lax.broadcasted_iota(jnp.int32, (128, 128), 1))
        - (TAPS * NFFT - 1)
    )
    ws, wc = sincos(odd & (8 * NFFT - 1), 8 * NFFT)
    shape = ws * wc / (odd.astype(jnp.float32) * (2.0 * math.pi / (8 * NFFT))) * (0.5 + 0.5 * wc)
    window[...] = shape
    total = jnp.sum(jnp.sum(shape * shape, axis=0, keepdims=True), axis=1, keepdims=True)
    scale = 0.25 * lax.rsqrt(total)

    for copy in small:
        copy.wait()

    lane = lax.broadcasted_iota(jnp.int32, (64, 128), 1)
    line = lax.broadcasted_iota(jnp.int32, (64, 128), 0)
    slot = line >> 5 << 1 | ((line >> 3) & 1)
    ahead = jnp.where(slot == 0, 2, jnp.where(slot == 1, 1 + 2 * zl, jnp.where(slot == 2, 3 - 2 * zl, 0)))
    channel = ((f + ahead) & 3) * 8 + ((line >> 2) & 1) * 4 + ((line >> 4) & 1) * 2 + ((line >> 1) & 1)
    kept_line = jnp.zeros((64, 128), jnp.int32)
    for j in range(32):
        kept_line = jnp.where(channel == j, kept[j], kept_line)
    quarter_turn = (line & 1) * (NFFT // 4)
    coarse_s, coarse_c = sincos((kept_line * (128 * (lane & 31)) + quarter_turn) & (NFFT - 1), NFFT)
    fine_s, fine_c = sincos((kept_line * lane) & (NFFT - 1), NFFT)

    def multiply(half, span):
        return lax.dot_general(
            frames[:, span], table[half * 256 : half * 256 + 256, span], NT, preferred_element_type=jnp.float32
        )

    partial = [0.0, 0.0]
    for part in range(CHUNKS):
        for a in range(part * CHUNK // 128, (part + 1) * CHUNK // 128):
            trig = coarse_c[:, a : a + 1] * fine_c - coarse_s[:, a : a + 1] * fine_s
            for t in range(TAPS):
                value = trig * window[t * 32 + a : t * 32 + a + 1, :]
                high = value.astype(jnp.bfloat16)
                low = (value - high.astype(jnp.float32)).astype(jnp.bfloat16)
                for quarter in range(4):
                    at = quarter // 2 * 256 + quarter % 2 * 64 + t * 16
                    table[at : at + 16, a * 128 : (a + 1) * 128] = high[quarter * 16 : quarter * 16 + 16]
                    table[at + 128 : at + 144, a * 128 : (a + 1) * 128] = low[quarter * 16 : quarter * 16 + 16]
        pltpu.make_async_copy(raw.at[part], raw.at[part], load_sem.at[part]).wait()
        span = slice(part * CHUNK, (part + 1) * CHUNK)
        for b in range(BLOCKS):
            frames[b * 16 : (b + 1) * 16, span] = raw[part, b].astype(jnp.float32).astype(jnp.bfloat16)
        if part < EARLY:
            continue
        span = slice(0 if part == EARLY else part * CHUNK, (part + 1) * CHUNK)
        for half in range(2 if part < CHUNKS - 1 else 1):
            partial[half] = partial[half] + multiply(half, span)

    row = lax.broadcasted_iota(jnp.int32, (16, 128), 0)
    gain = jnp.zeros((16, 128), jnp.int32)
    for j in range(16):
        gain = jnp.where(row == j, flags[j], gain)
    gain = gain.astype(jnp.float32) * scale

    def gather(half, product):
        product = product[:, :128] + product[:, 128:]
        lane = lax.broadcasted_iota(jnp.int32, (256, 128), 1)
        tap = (lane >> 4) & 3
        both = jnp.where(
            tap < 2,
            jnp.where(tap == 0, product[0:256], product[16:272]),
            jnp.where(tap == 2, product[32:288], product[48:304]),
        )
        for step in (32, 16):
            count = both.shape[0] // 2
            zero = (lax.broadcasted_iota(jnp.int32, (count, 128), 1) & step) == 0
            first, second = both[:count], both[count:]
            crossed = jnp.where(zero, second, first)
            crossed = jnp.where(zero, pltpu.roll(crossed, 128 - step, 1), pltpu.roll(crossed, step, 1))
            both = jnp.where(zero, first, second) + crossed
        tiles = [both[16 * j : 16 * j + 16] for j in range(4)]
        lane = lax.broadcasted_iota(jnp.int32, (16, 128), 1)
        for bit in range(2):
            step = 4 << bit
            zero = (lane & step) == 0
            for j in range(4):
                if j & (1 << bit):
                    continue
                first, second = tiles[j], tiles[j | (1 << bit)]
                tiles[j] = jnp.where(zero, first, pltpu.roll(second, step, 1))
                tiles[j | (1 << bit)] = jnp.where(zero, pltpu.roll(first, 128 - step, 1), second)
        for j in range(4):
            blocks[half * 2 + j // 2, j % 2] = tiles[j] * gain

    gather(0, partial[0])

    pl.semaphore_wait(barrier, len(greeted))

    def send(src, dst, send_sem, recv_sem, peer):
        pltpu.make_async_remote_copy(
            src_ref=src,
            dst_ref=dst,
            send_sem=send_sem,
            recv_sem=recv_sem,
            device_id=peer,
            device_id_type=MESH,
        ).start()

    def done(ref, sem):
        pltpu.make_async_copy(ref, ref, sem).wait()

    def done_blocks(counts, sem):
        for cc, count in enumerate(counts):
            width = max(n for n in range(1, 5) if count % n == 0)
            like = raw.at[0, 0 : count // width, :, 0 : 256 * width]
            if counts[0] == counts[1]:
                return done(like, sem)
            pl.when(core == cc)(functools.partial(done, like, sem))

    units = [tuple(pick((UNITS[0][j][n], UNITS[1][j][n])) for n in range(2)) for j in range(8)]
    spots = [lax.rem(z + 8 - dz, 8) for dz, _ in units]
    spots = [(lax.rem(zz, 2), source, lax.div(zz, 2)) for zz, (_, source) in zip(spots, units)]
    lines = [lax.rem(y + 4 - dy, 4) for dy in range(4)]

    def place(dy, j):
        return rows.at[(lines[dy], *spots[j])]

    mine = rows.at[y, zl, core, f]

    def hand_out(d):
        hosts = [next((cc, j) for cc in range(2) for j in range(8) if UNITS[cc][j] == (d, source)) for source in range(2)]
        host, j = pick((hosts[0][0], hosts[1][0])), pick((hosts[0][1], hosts[1][1]))
        block = blocks.at[SLOTS[d][0] + zl * (SLOTS[d][1] - SLOTS[d][0])]
        peer = on_z(d, host)
        send(block, mine, z_send, z_recv.at[j], peer)
        for dy in DIRECT.get(d, ()):
            on_y = {**peer, "xc": peer["xc"] - y * 4 + lax.rem(y + dy, 4) * 4}
            send(block, mine, z_send, y_recv.at[1 if dy == 2 else 0, j], on_y)

    for d in HALVES[0]:
        hand_out(d)
    gather(1, partial[1] + multiply(1, slice((CHUNKS - 1) * CHUNK, NFFT)))
    for d in HALVES[1]:
        hand_out(d)
    mine[...] = blocks[3]

    def to_columns(j):
        for d in (1, 3, 2):
            send(place(0, j), cols.at[r, spots[j][2]], x_send, x_recv, on_x(d, spots[j][1]))

    def where(j, test, act):
        passed = [test(UNITS[cc][j][0]) for cc in range(2)]
        if all(passed):
            act()
        elif any(passed):
            pl.when(core == passed.index(True))(act)

    def forward(j):
        block = place(0, j)

        for d, peer in y_peers.items():
            where(
                j,
                lambda dz: d not in DIRECT.get(dz, ()),
                lambda: send(block, block, y_send, y_recv.at[1 if d == 2 else 0, j], peer),
            )

    def share(dy, j):
        block = place(dy, j)
        send(block, block, c_send, c_recv, c_peer)

    forward(0)
    for kind, j in ARRIVALS:
        if kind == "z":
            done(place(0, j), z_recv.at[j])
            forward(j)
        elif kind == "pass":
            where(j, lambda dz: dz % 2 == 0, lambda: to_columns(j))
            share(0, j)
        elif kind == "near":
            done(raw.at[0, 0:2, :, 0:256], y_recv.at[0, j])
            share(1, j)
            share(3, j)
        else:
            done(raw.at[0, 0:1, :, 0:256], y_recv.at[1, j])
            share(2, j)
    done_blocks((12, 12), x_recv)
    done_blocks((32, 32), c_recv)
    for d in (0, 2, 6, 4):
        at = lax.div(lax.rem(z + 8 - d, 8), 2)
        cols[r, at] = rows[y, zl, core, at]
    done_blocks((7 + sum(map(len, DIRECT.values())),) * 2, z_send)
    done_blocks([sum(3 - len(DIRECT.get(dz, ())) for dz, _ in units) for units in UNITS], y_send)
    done_blocks([3 * sum(dz % 2 == 0 for dz, _ in units) for units in UNITS], x_send)
    done_blocks((32, 32), c_send)


def correlate(rows, cols, out, left, right, stage, out_sem):
    lane = lax.broadcasted_iota(jnp.int32, (256, 128), 1)
    long_lane = lax.broadcasted_iota(jnp.int32, (1024, 128), 1)
    real_lane = (lane & 1) == 0

    def write(channel, part):
        return pltpu.make_async_copy(stage.at[channel, part], out.at[channel, part], out_sem)

    for c_hi in range(2):
        x = rows[:, :, :, :, c_hi].reshape(1024, 128)
        turned = pltpu.roll(x, 64, 1)
        high = x.astype(jnp.bfloat16)
        left[c_hi, 0] = jnp.where(long_lane < 64, x, turned).astype(jnp.bfloat16)
        left[c_hi, 1] = jnp.where(long_lane < 64, turned, x).astype(jnp.bfloat16)
        left[c_hi, 2] = (x - high.astype(jnp.float32)).astype(jnp.bfloat16)
        c = cols[:, :, c_hi].reshape(256, 128) * (1.0 / SPEC)
        c_turned = pltpu.roll(c, 64, 1)
        for p in range(2):
            mine = (lane >> 6) == p
            operand = jnp.concatenate([left[c_hi, p], left[c_hi, 2]], axis=1)
            straight = jnp.where(mine, c, c_turned)
            swapped = jnp.where(real_lane, -pltpu.roll(straight, 127, 1), pltpu.roll(straight, 1, 1))
            for part, value in enumerate((straight, swapped)):
                value_high = value.astype(jnp.bfloat16).astype(jnp.float32)
                first = jnp.where(lane < 64, value_high, value - value_high)
                second = jnp.where(mine, value_high, 0.0)
                for e in range(2):
                    mask = ((lane >> 1) & 1) == e
                    channel = c_hi * 4 + p * 2 + e
                    right[channel, part] = jnp.concatenate(
                        [jnp.where(mask, first, 0.0), jnp.where(mask, second, 0.0)], axis=1
                    ).astype(jnp.bfloat16)
                    stage[channel, part] = lax.dot_general(
                        operand, right[channel, part], NT, preferred_element_type=jnp.float32
                    ).astype(jnp.bfloat16)
                    write(channel, part).start()
    pltpu.make_async_copy(stage, out, out_sem).wait()


def shards(samples, kept_channels, flags):
    vmem = pl.BlockSpec(memory_space=pltpu.VMEM)
    hbm = pl.BlockSpec(memory_space=pltpu.HBM)
    dma = pltpu.SemaphoreType.DMA
    rows, cols = pl.pallas_call(
        spread,
        out_shape=[pltpu.VMEM((4, 2, 2, 4, 2, 16, 128), jnp.float32), pltpu.VMEM((4, 4, 2, 16, 128), jnp.float32)],
        in_specs=[hbm, hbm, hbm],
        out_specs=[vmem, vmem],
        scratch_shapes=[
            pltpu.VMEM((CHUNKS, BLOCKS, 16, CHUNK), jnp.int32),
            pltpu.VMEM((BLOCKS * 16, NFFT), jnp.bfloat16),
            pltpu.VMEM((512, NFFT), jnp.bfloat16),
            pltpu.VMEM((128, 128), jnp.float32),
            pltpu.VMEM((4, 2, 16, 128), jnp.float32),
            pltpu.SMEM((32,), jnp.int32),
            pltpu.SMEM((16,), jnp.int32),
            dma((CHUNKS,)),
            dma((2,)),
            dma,
            dma((8,)),
            dma,
            dma((2, 8)),
            dma,
            dma,
            dma,
            dma,
        ],
        compiler_params=pltpu.CompilerParams(
            collective_id=0, has_side_effects=True, vmem_limit_bytes=40 * 1024 * 1024
        ),
        name="spread",
    )(*[pltpu.with_memory_space_constraint(array, pltpu.HBM) for array in (samples, kept_channels, flags)])
    return pl.pallas_call(
        correlate,
        out_shape=jax.ShapeDtypeStruct((8, 2, 1024, 256), jnp.bfloat16),
        in_specs=[vmem, vmem],
        out_specs=hbm,
        scratch_shapes=[
            pltpu.VMEM((2, 3, 1024, 128), jnp.bfloat16),
            pltpu.VMEM((8, 2, 256, 256), jnp.bfloat16),
            pltpu.VMEM((8, 2, 1024, 256), jnp.bfloat16),
            dma,
        ],
        compiler_params=pltpu.CompilerParams(vmem_limit_bytes=40 * 1024 * 1024),
        name="correlate",
    )(rows, cols)


def solution(mesh):
    return jax.shard_map(
        shards,
        mesh=mesh,
        in_specs=(P(("xr", "xc", "af"), None), P(), P(("xr", "xc", "af"))),
        out_specs=P("af", None, "xr", "xc"),
        check_vma=False,
    )
```

```python
import functools
import math

import jax
import jax.numpy as jnp
from jax import lax
from jax.experimental import pallas as pl
from jax.experimental.pallas import tpu as pltpu
from jax.sharding import PartitionSpec as P

NFFT = 4096
TAPS = 4
SPEC = 16
BLOCKS = SPEC + TAPS - 1
CHUNKS = 4
EARLY = 0
CHUNK = NFFT // CHUNKS
MESH = pl.DeviceIdType.MESH
NT = (((1,), (1,)), ((), ()))
UNITS = (
    ((0, 0), (7, 1), (1, 0), (7, 0), (6, 1), (2, 1), (6, 0), (2, 0)),
    ((0, 1), (1, 1), (3, 1), (5, 1), (3, 0), (5, 0), (4, 1), (4, 0)),
)
DIRECT = {1: (2, 1, 3), 7: (2, 1, 3), 2: (2,), 6: (2,)}
HALVES = ((4, 3, 5), (2, 6, 1, 7))
SLOTS = {4: (0, 0), 3: (1, 0), 5: (0, 1), 2: (1, 2), 6: (2, 1), 1: (3, 2), 7: (2, 3)}
ARRIVALS = (
    ("pass", 0), *(("z", j) for j in range(1, 8)), *(("pass", j) for j in (6, 7, 4, 5, 1, 2, 3)),
    *((kind, j) for j in range(8) for kind in ("near", "far")),
)


def sincos(phase, period):
    quarter = period // 4
    turned = phase + quarter // 2
    rest = (turned & (quarter - 1)) - quarter // 2
    quadrant = lax.shift_right_logical(turned, int(math.log2(quarter))) & 3
    angle = rest.astype(jnp.float32) * (2.0 * math.pi / period)
    z = angle * angle
    s = angle * (1.0 + z * (-1.0 / 6 + z * (1.0 / 120 + z * (-1.0 / 5040 + z * (1.0 / 362880)))))
    c = 1.0 + z * (-0.5 + z * (1.0 / 24 + z * (-1.0 / 720 + z * (1.0 / 40320))))
    odd = (quadrant & 1) == 1
    sine = jnp.where(odd, c, s)
    cosine = jnp.where(odd, s, c)
    sine = jnp.where(quadrant >= 2, -sine, sine)
    cosine = jnp.where((quadrant == 1) | (quadrant == 2), -cosine, cosine)
    return sine, cosine


def spread(
    samples, kept_hbm, flags_hbm, rows, cols, raw, frames, table, window, blocks, kept, flags,
    load_sem, small_sem, z_send, z_recv, y_send, y_recv, c_send, c_recv, x_send, x_recv,
):
    f, r, k = lax.axis_index("af"), lax.axis_index("xr"), lax.axis_index("xc")
    y, zl, core = lax.div(k, 4), lax.rem(lax.div(k, 2), 2), lax.rem(k, 2)
    z = f * 2 + zl

    small = [
        pltpu.make_async_copy(kept_hbm, kept, small_sem.at[0]),
        pltpu.make_async_copy(flags_hbm, flags, small_sem.at[1]),
    ]
    for copy in small:
        copy.start()
    for part in range(CHUNKS):
        for b in range(BLOCKS):
            pltpu.make_async_copy(
                samples.at[:, pl.ds(b * NFFT + part * CHUNK, CHUNK)], raw.at[part, b], load_sem.at[part]
            ).start()

    def pick(pair):
        return pair[0] if pair[0] == pair[1] else pair[0] + core * (pair[1] - pair[0])

    def on_z(d, cc):
        zz = lax.rem(z + d, 8)
        return {"af": lax.div(zz, 2), "xc": y * 4 + lax.rem(zz, 2) * 2 + cc}

    y_peers = {d: {"xc": lax.rem(y + d, 4) * 4 + zl * 2 + core} for d in (1, 3, 2)}
    c_peer = {"xc": k + 1 - 2 * core}

    def on_x(d, cc):
        return {"xr": lax.rem(r + d, 4), "xc": y * 4 + zl * 2 + cc}

    barrier = pltpu.get_barrier_semaphore()
    greeted = [on_z(d, cc) for d in range(1, 8) for cc in range(2)] + [on_x(d, cc) for d in range(1, 4) for cc in range(2)]
    greeted += [*y_peers.values(), c_peer]
    for d in sorted({*DIRECT, *(8 - d for d in DIRECT)}):
        for cc in range(2):
            for dy in sorted({*DIRECT.get(d, ()), *(4 - dy for dy in DIRECT.get(8 - d, ()))}):
                peer = on_z(d, cc)
                greeted.append({**peer, "xc": peer["xc"] - y * 4 + lax.rem(y + dy, 4) * 4})
    for peer in greeted:
        pl.semaphore_signal(barrier, inc=1, device_id=peer, device_id_type=MESH)

    odd = (
        2 * (lax.broadcasted_iota(jnp.int32, (128, 128), 0) * 128 + lax.broadcasted_iota(jnp.int32, (128, 128), 1))
        - (TAPS * NFFT - 1)
    )
    ws, wc = sincos(odd & (8 * NFFT - 1), 8 * NFFT)
    shape = ws * wc / (odd.astype(jnp.float32) * (2.0 * math.pi / (8 * NFFT))) * (0.5 + 0.5 * wc)
    window[...] = shape
    total = jnp.sum(jnp.sum(shape * shape, axis=0, keepdims=True), axis=1, keepdims=True)
    scale = 0.25 * lax.rsqrt(total)

    for copy in small:
        copy.wait()

    lane = lax.broadcasted_iota(jnp.int32, (64, 128), 1)
    line = lax.broadcasted_iota(jnp.int32, (64, 128), 0)
    slot = line >> 5 << 1 | ((line >> 3) & 1)
    ahead = jnp.where(slot == 0, 2, jnp.where(slot == 1, 1 + 2 * zl, jnp.where(slot == 2, 3 - 2 * zl, 0)))
    channel = ((f + ahead) & 3) * 8 + ((line >> 2) & 1) * 4 + ((line >> 4) & 1) * 2 + ((line >> 1) & 1)
    kept_line = jnp.zeros((64, 128), jnp.int32)
    for j in range(32):
        kept_line = jnp.where(channel == j, kept[j], kept_line)
    quarter_turn = (line & 1) * (NFFT // 4)
    coarse_s, coarse_c = sincos((kept_line * (128 * (lane & 31)) + quarter_turn) & (NFFT - 1), NFFT)
    fine_s, fine_c = sincos((kept_line * lane) & (NFFT - 1), NFFT)

    def multiply(half, span):
        return lax.dot_general(
            frames[:, span], table[half * 256 : half * 256 + 256, span], NT, preferred_element_type=jnp.float32
        )

    partial = [0.0, 0.0]
    for part in range(CHUNKS):
        for a in range(part * CHUNK // 128, (part + 1) * CHUNK // 128):
            trig = coarse_c[:, a : a + 1] * fine_c - coarse_s[:, a : a + 1] * fine_s
            for t in range(TAPS):
                value = trig * window[t * 32 + a : t * 32 + a + 1, :]
                high = value.astype(jnp.bfloat16)
                low = (value - high.astype(jnp.float32)).astype(jnp.bfloat16)
                for quarter in range(4):
                    at = quarter // 2 * 256 + quarter % 2 * 64 + t * 16
                    table[at : at + 16, a * 128 : (a + 1) * 128] = high[quarter * 16 : quarter * 16 + 16]
                    table[at + 128 : at + 144, a * 128 : (a + 1) * 128] = low[quarter * 16 : quarter * 16 + 16]
        pltpu.make_async_copy(raw.at[part], raw.at[part], load_sem.at[part]).wait()
        span = slice(part * CHUNK, (part + 1) * CHUNK)
        for b in range(BLOCKS):
            frames[b * 16 : (b + 1) * 16, span] = raw[part, b].astype(jnp.float32).astype(jnp.bfloat16)
        if part < EARLY:
            continue
        span = slice(0 if part == EARLY else part * CHUNK, (part + 1) * CHUNK)
        for half in range(2 if part < CHUNKS - 1 else 1):
            partial[half] = partial[half] + multiply(half, span)

    row = lax.broadcasted_iota(jnp.int32, (16, 128), 0)
    gain = jnp.zeros((16, 128), jnp.int32)
    for j in range(16):
        gain = jnp.where(row == j, flags[j], gain)
    gain = gain.astype(jnp.float32) * scale

    def gather(half, product):
        product = product[:, :128] + product[:, 128:]
        lane = lax.broadcasted_iota(jnp.int32, (256, 128), 1)
        tap = (lane >> 4) & 3
        both = jnp.where(
            tap < 2,
            jnp.where(tap == 0, product[0:256], product[16:272]),
            jnp.where(tap == 2, product[32:288], product[48:304]),
        )
        for step in (32, 16):
            count = both.shape[0] // 2
            zero = (lax.broadcasted_iota(jnp.int32, (count, 128), 1) & step) == 0
            first, second = both[:count], both[count:]
            crossed = jnp.where(zero, second, first)
            crossed = jnp.where(zero, pltpu.roll(crossed, 128 - step, 1), pltpu.roll(crossed, step, 1))
            both = jnp.where(zero, first, second) + crossed
        tiles = [both[16 * j : 16 * j + 16] for j in range(4)]
        lane = lax.broadcasted_iota(jnp.int32, (16, 128), 1)
        for bit in range(2):
            step = 4 << bit
            zero = (lane & step) == 0
            for j in range(4):
                if j & (1 << bit):
                    continue
                first, second = tiles[j], tiles[j | (1 << bit)]
                tiles[j] = jnp.where(zero, first, pltpu.roll(second, step, 1))
                tiles[j | (1 << bit)] = jnp.where(zero, pltpu.roll(first, 128 - step, 1), second)
        for j in range(4):
            blocks[half * 2 + j // 2, j % 2] = tiles[j] * gain

    gather(0, partial[0])

    pl.semaphore_wait(barrier, len(greeted))

    def send(src, dst, send_sem, recv_sem, peer):
        pltpu.make_async_remote_copy(
            src_ref=src,
            dst_ref=dst,
            send_sem=send_sem,
            recv_sem=recv_sem,
            device_id=peer,
            device_id_type=MESH,
        ).start()

    def done(ref, sem):
        pltpu.make_async_copy(ref, ref, sem).wait()

    def done_blocks(counts, sem):
        for cc, count in enumerate(counts):
            width = max(n for n in range(1, 5) if count % n == 0)
            like = raw.at[0, 0 : count // width, :, 0 : 256 * width]
            if counts[0] == counts[1]:
                return done(like, sem)
            pl.when(core == cc)(functools.partial(done, like, sem))

    units = [tuple(pick((UNITS[0][j][n], UNITS[1][j][n])) for n in range(2)) for j in range(8)]
    spots = [lax.rem(z + 8 - dz, 8) for dz, _ in units]
    spots = [(lax.rem(zz, 2), source, lax.div(zz, 2)) for zz, (_, source) in zip(spots, units)]
    lines = [lax.rem(y + 4 - dy, 4) for dy in range(4)]

    def place(dy, j):
        return rows.at[(lines[dy], *spots[j])]

    mine = rows.at[y, zl, core, f]

    def hand_out(d):
        hosts = [next((cc, j) for cc in range(2) for j in range(8) if UNITS[cc][j] == (d, source)) for source in range(2)]
        host, j = pick((hosts[0][0], hosts[1][0])), pick((hosts[0][1], hosts[1][1]))
        block = blocks.at[SLOTS[d][0] + zl * (SLOTS[d][1] - SLOTS[d][0])]
        peer = on_z(d, host)
        send(block, mine, z_send, z_recv.at[j], peer)
        for dy in DIRECT.get(d, ()):
            on_y = {**peer, "xc": peer["xc"] - y * 4 + lax.rem(y + dy, 4) * 4}
            send(block, mine, z_send, y_recv.at[1 if dy == 2 else 0, j], on_y)

    for d in HALVES[0]:
        hand_out(d)
    gather(1, partial[1] + multiply(1, slice((CHUNKS - 1) * CHUNK, NFFT)))
    for d in HALVES[1]:
        hand_out(d)
    mine[...] = blocks[3]

    def to_columns(j):
        for d in (1, 3, 2):
            send(place(0, j), cols.at[r, spots[j][2]], x_send, x_recv, on_x(d, spots[j][1]))

    def where(j, test, act):
        passed = [test(UNITS[cc][j][0]) for cc in range(2)]
        if all(passed):
            act()
        elif any(passed):
            pl.when(core == passed.index(True))(act)

    def forward(j):
        block = place(0, j)

        for d, peer in y_peers.items():
            where(
                j,
                lambda dz: d not in DIRECT.get(dz, ()),
                lambda: send(block, block, y_send, y_recv.at[1 if d == 2 else 0, j], peer),
            )

    def share(dy, j):
        block = place(dy, j)
        send(block, block, c_send, c_recv, c_peer)

    forward(0)
    for kind, j in ARRIVALS:
        if kind == "z":
            done(place(0, j), z_recv.at[j])
            forward(j)
        elif kind == "pass":
            where(j, lambda dz: dz % 2 == 0, lambda: to_columns(j))
            share(0, j)
        elif kind == "near":
            done(raw.at[0, 0:2, :, 0:256], y_recv.at[0, j])
            share(1, j)
            share(3, j)
        else:
            done(raw.at[0, 0:1, :, 0:256], y_recv.at[1, j])
            share(2, j)
    done_blocks((12, 12), x_recv)
    done_blocks((32, 32), c_recv)
    for d in (0, 2, 6, 4):
        at = lax.div(lax.rem(z + 8 - d, 8), 2)
        cols[r, at] = rows[y, zl, core, at]
    done_blocks((7 + sum(map(len, DIRECT.values())),) * 2, z_send)
    done_blocks([sum(3 - len(DIRECT.get(dz, ())) for dz, _ in units) for units in UNITS], y_send)
    done_blocks([3 * sum(dz % 2 == 0 for dz, _ in units) for units in UNITS], x_send)
    done_blocks((32, 32), c_send)


def correlate(rows, cols, out, left, right, stage, out_sem):
    lane = lax.broadcasted_iota(jnp.int32, (256, 128), 1)
    real_lane = (lane & 1) == 0

    def prepare_columns(c_hi, p):
        c = cols[:, :, c_hi].reshape(256, 128) * (1.0 / SPEC)
        mine = (lane >> 6) == p
        straight = jnp.where(mine, c, pltpu.roll(c, 64, 1))
        swapped = jnp.where(real_lane, -pltpu.roll(straight, 127, 1), pltpu.roll(straight, 1, 1))
        for part, value in enumerate((straight, swapped)):
            value_high = value.astype(jnp.bfloat16).astype(jnp.float32)
            first = jnp.where(lane < 64, value_high, value - value_high)
            second = jnp.where(mine, value_high, 0.0)
            for e in range(2):
                mask = ((lane >> 1) & 1) == e
                right[c_hi * 4 + p * 2 + e, part] = jnp.concatenate(
                    [jnp.where(mask, first, 0.0), jnp.where(mask, second, 0.0)], axis=1
                ).astype(jnp.bfloat16)

    def prepare_rows(c_hi, line):
        x = rows[line, :, :, :, c_hi].reshape(256, 128)
        turned = pltpu.roll(x, 64, 1)
        high = x.astype(jnp.bfloat16)
        at = slice(line * 256, line * 256 + 256)
        left[c_hi, 0, at] = jnp.where(lane < 64, x, turned).astype(jnp.bfloat16)
        left[c_hi, 1, at] = jnp.where(lane < 64, turned, x).astype(jnp.bfloat16)
        left[c_hi, 2, at] = (x - high.astype(jnp.float32)).astype(jnp.bfloat16)

    def multiply(c_hi, p, at):
        operand = jnp.concatenate([left[c_hi, p, at], left[c_hi, 2, at]], axis=1)
        for e in range(2):
            for part in range(2):
                channel = c_hi * 4 + p * 2 + e
                stage[channel, part, at] = lax.dot_general(
                    operand, right[channel, part], NT, preferred_element_type=jnp.float32
                ).astype(jnp.bfloat16)
                pltpu.make_async_copy(stage.at[channel, part, at], out.at[channel, part, at], out_sem).start()

    for c_hi in range(2):
        prepare_columns(c_hi, 0)
        for line in range(4):
            prepare_rows(c_hi, line)
            multiply(c_hi, 0, slice(line * 256, line * 256 + 256))
        prepare_columns(c_hi, 1)
        multiply(c_hi, 1, slice(0, 1024))
    pltpu.make_async_copy(stage, out, out_sem).wait()


def shards(samples, kept_channels, flags):
    vmem = pl.BlockSpec(memory_space=pltpu.VMEM)
    hbm = pl.BlockSpec(memory_space=pltpu.HBM)
    dma = pltpu.SemaphoreType.DMA
    rows, cols = pl.pallas_call(
        spread,
        out_shape=[pltpu.VMEM((4, 2, 2, 4, 2, 16, 128), jnp.float32), pltpu.VMEM((4, 4, 2, 16, 128), jnp.float32)],
        in_specs=[hbm, hbm, hbm],
        out_specs=[vmem, vmem],
        scratch_shapes=[
            pltpu.VMEM((CHUNKS, BLOCKS, 16, CHUNK), jnp.int32),
            pltpu.VMEM((BLOCKS * 16, NFFT), jnp.bfloat16),
            pltpu.VMEM((512, NFFT), jnp.bfloat16),
            pltpu.VMEM((128, 128), jnp.float32),
            pltpu.VMEM((4, 2, 16, 128), jnp.float32),
            pltpu.SMEM((32,), jnp.int32),
            pltpu.SMEM((16,), jnp.int32),
            dma((CHUNKS,)),
            dma((2,)),
            dma,
            dma((8,)),
            dma,
            dma((2, 8)),
            dma,
            dma,
            dma,
            dma,
        ],
        compiler_params=pltpu.CompilerParams(
            collective_id=0, has_side_effects=True, vmem_limit_bytes=40 * 1024 * 1024
        ),
        name="spread",
    )(*[pltpu.with_memory_space_constraint(array, pltpu.HBM) for array in (samples, kept_channels, flags)])
    return pl.pallas_call(
        correlate,
        out_shape=jax.ShapeDtypeStruct((8, 2, 1024, 256), jnp.bfloat16),
        in_specs=[vmem, vmem],
        out_specs=hbm,
        scratch_shapes=[
            pltpu.VMEM((2, 3, 1024, 128), jnp.bfloat16),
            pltpu.VMEM((8, 2, 256, 256), jnp.bfloat16),
            pltpu.VMEM((8, 2, 1024, 256), jnp.bfloat16),
            dma,
        ],
        compiler_params=pltpu.CompilerParams(vmem_limit_bytes=40 * 1024 * 1024),
        name="correlate",
    )(rows, cols)


def solution(mesh):
    return jax.shard_map(
        shards,
        mesh=mesh,
        in_specs=(P(("xr", "xc", "af"), None), P(), P(("xr", "xc", "af"))),
        out_specs=P("af", None, "xr", "xc"),
        check_vma=False,
    )
```
